256 devices in a mesh: dp: 32 (over y_hi, z, core), tensor: 8 (over y_lo, x).
Axes of the slice: x: 4, y: 4 (y_hi: 2, y_lo: 2; y = y_hi * 2 + y_lo), z: 8, core: 2. Of those that a mesh axis runs over, the one named last changes fastest.
Arguments:
- roll_x: bfloat16 [512, 8192], P('dp', 'tensor'), may hold values from -6 to 6
- queries: bfloat16 [512, 8192], P('dp', 'tensor'), may hold values from -128 to 128, as said below
- cache_k: bfloat16 [512, 256, 1024], P('dp', None, 'tensor'), may hold values from -4 to 4
- cache_v: bfloat16 [512, 256, 1024], P('dp', None, 'tensor'), may hold values from -6 to 6
- cache_len: int32 [512], P('dp'), may hold values from 2 to 256
- tenant_roll: int32 [512], P('dp'), may hold values from 0 to 63
- w_key: bfloat16 [8192, 1024], P(None, 'tensor'), may hold values from -0.0625 to 0.0625
- w_value: bfloat16 [8192, 1024], P(None, 'tensor'), may hold values from -0.0625 to 0.0625
- ia3_key: float32 [64, 1024], replicated, may hold values from 0.25 to 1.75
- ia3_value: float32 [64, 1024], replicated, may hold values from 0.25 to 1.75
- train_x: bfloat16 [65536, 8192], P(('dp', 'tensor')), may hold values from -6 to 6
- upstream: bfloat16 [65536, 1024], P(('dp', 'tensor')), may hold values from -24 to 24
- tenant_train: int32 [65536], P(('dp', 'tensor')), may hold values from 0 to 63, as said below
- advantage: int32 [65536], P(('dp', 'tensor')), may hold values from -3 to 3
Outputs:
- attn_out: bfloat16 [512, 8192], P('dp', 'tensor')
- grad_ia3_value: float32 [64, 1024], P('dp', 'tensor')
- tenant_loss: float32 [64], replicated
The draws below stay inside these ranges and needn't reach their ends.
Inputs may be any that keep to these rules, and one draw needn't show every extreme that they name: `queries`: query entries lie within the stated range. `tenant_train`: some tenants have no scored tokens.
All inputs are finite; a program needn't handle non-finite values.
Results may differ from the reference program's by a relative error of at most 0.0055.
Values may be sent and summed in bfloat16 or wider, within the bound.
A program may use at most 128 MiB of HBM per device.

```python
import jax
import jax.numpy as jnp
from jax import lax

D = 8192
HEADS = 64
KV_HEADS = 8
HD = 128
TENANTS = 64
CACHE = 256
GROUP = 8
KVD = 1024
ROWS = 512
TOKENS = 65536


def shared_cache(key):
    cached = jnp.clip(jax.random.normal(jax.random.fold_in(key, 11), (ROWS, CACHE, KVD), jnp.float32), -4.0, 4.0)
    return cached


def draw_cache_k(key, part):
    return shared_cache(key).astype(jnp.bfloat16)


def draw_queries(key, part):
    base = jnp.clip(jax.random.normal(jax.random.fold_in(key, 12), (ROWS, HEADS * HD), jnp.float32), -6.0, 6.0)
    return base.astype(jnp.bfloat16)


def draw_tenant_train(key, part):
    live = TENANTS - TENANTS // 8
    order = jax.random.permutation(jax.random.fold_in(key, 21), TENANTS).astype(jnp.int32)
    reach = jax.random.randint(jax.random.fold_in(key, 22), (TOKENS,), 1, live + 1, dtype=jnp.int32)
    ranked = jax.random.randint(jax.random.fold_in(key, 23), (TOKENS,), 0, reach, dtype=jnp.int32)
    return order[ranked].astype(jnp.int32)


def place_ends(values, stream_key, low, largest):
    spot = [jax.random.randint(jax.random.fold_in(stream_key, axis), (), 0, length) for axis, length in enumerate(values.shape)]
    main_axis = values.shape.index(max(values.shape))
    next_to = spot[:main_axis] + [(spot[main_axis] + 1) % values.shape[main_axis]] + spot[main_axis + 1:]
    return values.at[tuple(spot)].set(low).at[tuple(next_to)].set(largest)


def block_levels(own_key, dims, shards, least, top_value):
    def one(axis_at, parts):
        draws = jax.random.uniform(jax.random.fold_in(jax.random.fold_in(own_key, 6), axis_at), (parts,), jnp.float32, least / len(shards), top_value / len(shards))
        return jnp.repeat(jnp.exp(draws), dims[axis_at] // parts).reshape((-1,) + (1,) * (len(dims) - axis_at - 1))

    loudness = one(*shards[0])
    for cut in shards[1:]:
        loudness = loudness * one(*cut)
    return loudness


def centred(rng, shape, deviation, bound, shards=(), held_as=jnp.bfloat16):
    drawn = jax.random.normal(rng, shape, jnp.float32) * deviation
    if len(shards) > 0:
        drawn = block_levels(rng, shape, shards, -0.22, 0.18) * drawn
    return jnp.clip(drawn, min=-bound, max=bound).astype(held_as)


def setup_inputs(seed: int = 0) -> dict:
    key_of = jax.random.split(jax.random.key(seed), 15)
    return {
        "roll_x": centred(key_of[0], (ROWS, D), 1.0, 6.0, ((0, 32), (1, 8))),
        "queries": draw_queries(jax.random.fold_in(key_of[14], 71), 0),
        "cache_k": draw_cache_k(jax.random.fold_in(key_of[14], 71), 0),
        "cache_v": centred(key_of[3], (ROWS, CACHE, KVD), 1.0, 6.0, ((0, 32), (2, 8))),
        "cache_len": place_ends(jax.random.randint(key_of[4], (ROWS,), 2, CACHE + 1), jax.random.fold_in(key_of[4], 1), 2, CACHE).astype(jnp.int32),
        "tenant_roll": place_ends(jax.random.randint(key_of[5], (ROWS,), 0, TENANTS), jax.random.fold_in(key_of[5], 1), 0, TENANTS - 1).astype(jnp.int32),
        "w_key": centred(key_of[6], (D, KVD), D ** -0.5, 0.0625, ((1, 8),)),
        "w_value": centred(key_of[7], (D, KVD), D ** -0.5, 0.0625, ((1, 8),)),
        "ia3_key": jnp.clip(1.0 + 0.15 * jax.random.normal(key_of[8], (TENANTS, KVD), jnp.float32), 0.25, 1.75),
        "ia3_value": jnp.clip(1.0 + 0.15 * jax.random.normal(key_of[9], (TENANTS, KVD), jnp.float32), 0.25, 1.75),
        "train_x": centred(key_of[10], (TOKENS, D), 1.0, 6.0, ((0, 256),)),
        "upstream": centred(key_of[11], (TOKENS, KVD), 4.0, 24.0, ((0, 256),)),
        "tenant_train": draw_tenant_train(jax.random.fold_in(key_of[14], 71), 0),
        "advantage": place_ends(jax.random.randint(key_of[13], (TOKENS,), -3, 4), jax.random.fold_in(key_of[13], 1), -3, 3).astype(jnp.int32),
    }


def tenant_table(tenant):
    return (tenant[:, None] == jnp.arange(TENANTS, dtype=jnp.int32)[None, :]).astype(jnp.float32)

def reference(roll_x, queries, cache_k, cache_v, cache_len, tenant_roll, w_key, w_value, ia3_key, ia3_value, train_x, upstream, tenant_train, advantage):
    high = lax.Precision.HIGHEST
    onehot_roll = tenant_table(tenant_roll)
    key_gain = jnp.dot(onehot_roll, ia3_key, precision=high)
    value_gain = jnp.dot(onehot_roll, ia3_value, precision=high)
    key_new = (jnp.dot(roll_x, w_key, preferred_element_type=jnp.float32) * key_gain).astype(jnp.bfloat16)
    value_new = (jnp.dot(roll_x, w_value, preferred_element_type=jnp.float32) * value_gain).astype(jnp.bfloat16)
    scale_factor = 1.0 / jnp.sqrt(jnp.float32(HD))
    query_all = queries.astype(jnp.float32).reshape(ROWS, KV_HEADS, GROUP, HD)
    in_cache = (jnp.arange(CACHE, dtype=jnp.int32)[None, :] < cache_len[:, None])[:, None, :]
    pieces_out = []
    for kv_head in range(KV_HEADS):
        lower = kv_head * HD
        key_cache = cache_k[:, :, lower:lower + HD].astype(jnp.float32)
        value_cache = cache_v[:, :, lower:lower + HD].astype(jnp.float32)
        key_own = key_new[:, lower:lower + HD].astype(jnp.float32)
        value_own = value_new[:, lower:lower + HD].astype(jnp.float32)
        query_head = query_all[:, kv_head]
        scores = jnp.einsum('rgd,rcd->rgc', query_head, key_cache) * scale_factor
        scores = jnp.where(in_cache, scores, -jnp.inf)
        new_score = jnp.einsum('rgd,rd->rg', query_head, key_own) * scale_factor
        highest = jnp.maximum(lax.optimization_barrier(jnp.max(scores, axis=-1)), new_score)
        expo = jnp.exp(scores - highest[..., None])
        expo_new = jnp.exp(new_score - highest)
        denominator = lax.optimization_barrier(jnp.sum(expo, axis=-1)) + expo_new
        weights = (expo / denominator[..., None]).astype(jnp.bfloat16).astype(jnp.float32)
        weight_new = (expo_new / denominator).astype(jnp.bfloat16).astype(jnp.float32)
        result = jnp.einsum('rgc,rcd->rgd', weights, value_cache) + weight_new[..., None] * value_own[:, None, :]
        pieces_out.append(result.reshape(ROWS, GROUP * HD))
    attn_out = jnp.concatenate(pieces_out, axis=1).astype(jnp.bfloat16)
    values = jnp.dot(train_x, w_value, preferred_element_type=jnp.float32)
    onehot_train = tenant_table(tenant_train)
    counts = lax.optimization_barrier(jnp.sum(onehot_train, axis=0))
    divisor = jnp.maximum(counts, 1.0)
    weighted = advantage.astype(jnp.float32)[:, None] * upstream.astype(jnp.float32) * values
    sums = jnp.dot(onehot_train.T, weighted, precision=high)
    gain_rows = jnp.dot(onehot_train, ia3_value, precision=high)
    loss_sums = jnp.dot(onehot_train.T, lax.optimization_barrier(jnp.sum(weighted * gain_rows, axis=1)), precision=high)
    return (attn_out, -sums / divisor[:, None], -loss_sums / divisor)
```

```python
import jax
import jax.numpy as jnp
from jax import lax
from jax.experimental import pallas as pl
from jax.experimental.pallas import tpu as pltpu
from jax.sharding import Mesh
from jax.sharding import PartitionSpec as P

HD = 128
TENANTS = 64
AXES = ("y_hi", "z", "core", "y_lo", "x")
DP = ("y_hi", "z", "core")
TENSOR = ("y_lo", "x")
DP_TENSOR = DP + TENSOR
MESH = pl.DeviceIdType.MESH
F32 = jnp.float32
BF16 = jnp.bfloat16

O, XM, XP, X2, F0, FM, FP, F2 = range(8)
SHIFT = ((0, 0), (0, 3), (0, 1), (0, 2), (1, 0), (1, 3), (1, 1), (1, 2))
INVERSE = (O, XP, XM, X2, F0, FP, FM, F2)

HALF = 4096
ZROWS = 1024
QROWS = (HALF - ZROWS) // 4
ZHALF = ZROWS // 2

FROM_XM = ((XM, 0), (XM, 1), (XM, 2), (X2, 0), (X2, 2), (XM, 3), (FM, 3))
FROM_XP = ((XP, 0), (XP, 1), (XP, 3), (X2, 1), (X2, 3), (XP, 2), (FP, 2))
FROM_YM = ((F0, 0), (F0, 2), (FM, 0), (FM, 1), (FM, 2), (F2, 0), (F2, 2))
FROM_YP = ((F0, 1), (F0, 3), (FP, 0), (FP, 1), (FP, 3), (F2, 1), (F2, 3))
LINKS = (FROM_XM, FROM_XP, FROM_YM, FROM_YP)
SENT_AS = (
    {XM: O, X2: XM, FM: F0},
    {XP: O, X2: XP, FP: F0},
    {F0: O, FM: XM, FP: XP, F2: X2},
    {F0: O, FM: XM, FP: XP, F2: X2},
)
Z_SEND = {0: (F0,), 1: (XM, XP), 3: (X2, FM, FP), 5: (F2,)}
Z_TAKE = {2: (F0,), 3: (XM,), 4: (XP,), 5: (X2,), 6: (FM, FP, F2)}
COMPLETE = {2: (F0,), 5: (XM, XP, X2), 6: (FM, FP, F2)}


def dot(a, b):
    return jnp.dot(a, b, preferred_element_type=F32)


def exact_dot(a, b, dims):
    return lax.dot_general(
        a, b, (dims, ((), ())), precision=lax.Precision.HIGHEST, preferred_element_type=F32
    )


def kernel(
    clen, troll, roll_h, q_h, ck_h, cv_h, wk_h, wv_h, ik_h, iv_h, x_h, up_h, tt_h, adv_h,
    attn_o, grad_o, loss_o,
    wbuf, wv, wk, xh, up, kc, vc, q, rx, ik, iv, tt, adv, acc, pbuf, sbuf, gbuf, lmine, lbuf,
    msg, rbuf, qs, sc, mix, snew, mt, lacc, cnt,
    lsem, wsend, wrecv, zrecv, xsend, xrecv, rsend, rrecv, psend, precv, gsend, grecv,
    lsend, lrecv, msend, mrecv,
):
    y_hi, z, core, y_lo, x = (lax.axis_index(a) for a in AXES)
    d = y_hi * 16 + z * 2 + core
    t = y_lo * 4 + x
    odd = z % 2
    y = 2 * y_hi + y_lo
    y_up, y_down = (y + 1) % 4, (y + 3) % 4
    me = (y_hi, z, core, y_lo, x)
    sibling = (y_hi, z, 1 - core, y_lo, x)
    z_up = (y_hi, (z + 1) % 8, core, y_lo, x)
    z_down = (y_hi, (z + 7) % 8, core, y_lo, x)
    to_link = (
        (y_hi, z, core, y_lo, (x + 1) % 4),
        (y_hi, z, core, y_lo, (x + 3) % 4),
        (y_up // 2, z, core, y_up % 2, x),
        (y_down // 2, z, core, y_down % 2, x),
    )

    def place(block):
        return (y_lo + SHIFT[block][0]) % 2, (x + SHIFT[block][1]) % 4

    def peer(block):
        py, px = place(block)
        return (y_hi, z, core, py, px)

    def columns(block):
        py, px = place(block)
        return pl.ds(pl.multiple_of((py * 4 + px) * HD, HD), HD)

    def dp_peer(step):
        other = (d + step) % 32
        return other, (other // 16, (other // 2) % 8, other % 2, y_lo, x)

    def remote(src, dst, send, recv, device):
        return pltpu.make_async_remote_copy(
            src_ref=src, dst_ref=dst, send_sem=send, recv_sem=recv,
            device_id=device, device_id_type=MESH,
        )

    own_half = pl.ds(pl.multiple_of(core * HALF, HALF), HALF)
    other_half = pl.ds(pl.multiple_of((1 - core) * HALF, HALF), HALF)
    local = [
        pltpu.make_async_copy(src, dst, lsem.at[k])
        for k, (src, dst) in enumerate(
            (
                (wv_h, wv),
                (x_h.at[:, own_half], xh.at[pl.ds(0, 256)]),
                (tt_h, tt),
                (adv_h, adv),
                (up_h, up),
                (wk_h, wk),
                (roll_h, rx.at[t]),
                (ik_h.at[:, pl.ds(pl.multiple_of(t * HD, HD), HD)], ik),
                (iv_h, iv),
                (q_h, q),
                (ck_h, kc),
                (cv_h, vc),
            )
        )
    ]
    for copy in local:
        copy.start()

    barrier = pltpu.get_barrier_semaphore()

    def greet(step, carry):
        pl.semaphore_signal(barrier, inc=1, device_id=dp_peer(step)[1], device_id_type=MESH)
        return carry

    for block in range(1, 8):
        pl.semaphore_signal(barrier, inc=1, device_id=peer(block), device_id_type=MESH)
    pl.semaphore_signal(
        barrier, inc=1, device_id=(1 - y_hi, z, core, 1 - y_lo, x), device_id_type=MESH
    )
    lax.fori_loop(1, 32, greet, 0)
    pl.semaphore_wait(barrier, 39)

    def quarter(k):
        return pl.multiple_of(
            (1 - odd) * (k * QROWS) + odd * (HALF - (k + 1) * QROWS), 64
        )

    def link_copy(link, r):
        block, k = LINKS[link][r]
        source = SENT_AS[link][block]
        row = quarter(k)
        if source == O:
            src = wv_h.at[pl.ds(pl.multiple_of(core * HALF + row, 64), QROWS)]
        else:
            src = wbuf.at[source - 1, pl.ds(row, QROWS)]
        return remote(
            src, wbuf.at[block - 1, pl.ds(row, QROWS)], wsend, wrecv.at[link, r], to_link[link]
        )

    def z_copy(block, h, base):
        rows = pl.ds(pl.multiple_of(base + h * ZHALF, 64), ZHALF)
        ref = wbuf.at[block - 1, rows]
        return remote(ref, ref, wsend, zrecv.at[h, block - 1], z_up if h == 0 else z_down)

    z_sent = odd * (HALF - ZROWS)
    z_taken = (1 - odd) * (HALF - ZROWS)

    def issue(r):
        for link in range(4):
            link_copy(link, r).start()

    roll_sends = [
        remote(roll_h, rx.at[t], rsend, rrecv, peer(block)) for block in range(1, 8)
    ]
    x_copy = remote(x_h.at[:, other_half], xh.at[pl.ds(256, 256)], xsend, xrecv, sibling)
    issue(0)
    x_copy.start()
    for copy in roll_sends:
        copy.start()
    issue(1)

    def product(block, row, length, first=False):
        if block == O:
            part = wv[pl.ds(pl.multiple_of(core * HALF + row, 64), length), :]
        else:
            part = wbuf[block - 1, pl.ds(row, length), :]
        new = dot(xh[:, pl.ds(pl.multiple_of(row, 64), length)], part)
        if first:
            acc[block] = new
        else:
            acc[block] += new

    def partial_copy(block):
        return remote(
            acc.at[block, pl.ds(256, 256)], pbuf.at[block], psend, precv.at[block], sibling
        )

    def sum_copy(block):
        return remote(
            sbuf.at[block], gbuf.at[INVERSE[block] - 1], gsend, grecv, peer(block)
        )

    def finish(block, first=False):
        partial_copy(block).wait_recv()
        values = acc[block, 0:256, :] + pbuf[block]
        weighted = values * up[:, columns(block)].astype(F32)
        high = weighted.astype(BF16)
        low = (weighted - high.astype(F32)).astype(BF16)
        sums = dot(mt[...], high) + dot(mt[...], low)
        sbuf[block] = sums
        if block != O:
            sum_copy(block).start()
        part = sums * iv[:, columns(block)]
        if first:
            lacc[0:64, :] = part
        else:
            lacc[0:64, :] += part

    for k in (2, 3):
        local[k].wait()
    tenant = lax.broadcasted_iota(jnp.int32, (64, 128), 0)
    hits = [
        (tenant == jnp.broadcast_to(tt[k : k + 1, :], (64, 128))).astype(F32) for k in range(2)
    ]
    for k in range(2):
        gain = jnp.broadcast_to(adv[k : k + 1, :].astype(F32), (64, 128))
        mt[:, k * 128 : (k + 1) * 128] = (hits[k] * gain).astype(BF16)
    cnt[0:64, :] = hits[0] + hits[1]
    cnt[64:128, :] = jnp.zeros((64, 128), F32)
    lacc[64:128, :] = jnp.zeros((64, 128), F32)

    scale = 1.0 / jnp.sqrt(F32(HD))

    def spread(h, transposed=False):
        shape = (16, 128) if transposed else (128, 16)
        pair = lax.broadcasted_iota(jnp.int32, shape, 1 if transposed else 0)
        row = lax.broadcasted_iota(jnp.int32, shape, 0 if transposed else 1)
        if h is None:
            return (pair // 8 == row).astype(F32).astype(BF16)
        return (pair == row * 8 + h).astype(F32).astype(BF16)

    def project():
        for k in (5, 6, 7, 8, 9):
            local[k].wait()
        remote(rx.at[pl.ds(0, 7)], rx.at[pl.ds(0, 7)], rsend, rrecv, sibling).wait_recv()
        key_sum = jnp.zeros((16, HD), F32)
        value_sum = jnp.zeros((16, HD), F32)
        for k in range(8):
            part = rx[k]
            key_sum = key_sum + dot(part, wk[k * 1024 : (k + 1) * 1024, :])
            value_sum = value_sum + dot(part, wv[k * 1024 : (k + 1) * 1024, :])
        row = lax.broadcasted_iota(jnp.int32, (16, TENANTS), 0)
        owner = jnp.zeros((16, TENANTS), jnp.int32)
        for r in range(16):
            owner = jnp.where(row == r, troll[r], owner)
        onehot = (owner == lax.broadcasted_iota(jnp.int32, (16, TENANTS), 1)).astype(F32)
        key_gain = exact_dot(onehot, ik[...], ((1,), (0,)))
        value_gain = exact_dot(onehot, iv[:, columns(O)], ((1,), (0,)))
        key_new = (key_sum * key_gain).astype(BF16)
        value_new = (value_sum * value_gain).astype(BF16)
        queries = jnp.zeros((128, HD), F32)
        for h in range(8):
            queries = queries + dot(spread(h), q[:, h * HD : (h + 1) * HD])
        qs[...] = queries
        each = spread(None)
        snew[...] = jnp.broadcast_to(
            jnp.sum(queries * dot(each, key_new), axis=1, keepdims=True) * scale, (128, 128)
        )
        mix[...] = dot(each, value_new)

    def score():
        local[10].wait()
        place_in_cache = lax.broadcasted_iota(jnp.int32, (8, 256), 1)
        for r in range(16):
            s = lax.dot_general(
                qs[r * 8 : (r + 1) * 8, :].astype(BF16), kc[r], (((1,), (1,)), ((), ())),
                preferred_element_type=F32,
            ) * scale
            sc[r * 8 : (r + 1) * 8, :] = jnp.where(place_in_cache < clen[r], s, -jnp.inf)

    def normalise():
        s = sc[...]
        new = snew[:, 0:1]
        highest = jnp.maximum(jnp.max(s, axis=1, keepdims=True), new)
        expo = jnp.exp(s - highest)
        expo_new = jnp.exp(new - highest)
        denominator = jnp.sum(expo, axis=1, keepdims=True) + expo_new
        sc[...] = (expo / denominator).astype(BF16).astype(F32)
        mix[...] = (expo_new / denominator).astype(BF16).astype(F32) * mix[...]

    def mixture():
        local[11].wait()
        for r in range(16):
            rows = slice(r * 8, (r + 1) * 8)
            mix[rows, :] += dot(sc[rows, :].astype(BF16), vc[r])
        mixed = mix[...].astype(BF16)
        for h in range(8):
            attn_o[:, h * HD : (h + 1) * HD] = dot(spread(h, True), mixed).astype(BF16)

    beside = {0: project, 1: score, 2: normalise, 3: mixture}

    for k in (0, 1, 4):
        local[k].wait()
    x_copy.wait_recv()
    for k in range(4):
        product(O, k * 1024, 1024, k == 0)
    partial_copy(O).start()

    seen = {O}
    for r in range(7):
        for link in range(4):
            link_copy(link, r).wait_recv()
        if r + 2 < 7:
            issue(r + 2)
        for block in Z_SEND.get(r, ()):
            for h in range(2):
                z_copy(block, h, z_sent).start()
        for link in range(4):
            block, k = LINKS[link][r]
            product(block, quarter(k), QROWS, block not in seen)
            seen.add(block)
        for block in Z_TAKE.get(r, ()):
            for h in range(2):
                z_copy(block, h, z_taken).wait_recv()
            product(block, pl.multiple_of(z_taken, 64), ZROWS)
        for block in COMPLETE.get(r, ()):
            partial_copy(block).start()
        if r in beside:
            beside[r]()
        if r == 1:
            finish(O, True)
        if r == 3:
            finish(F0)
        if r == 5:
            for block in COMPLETE[5]:
                finish(block)
    for block in COMPLETE[6]:
        finish(block)

    ones = jnp.ones((8, 128), F32)
    tile_row = lax.broadcasted_iota(jnp.int32, (8, 128), 0)
    loss_row = exact_dot(ones, lacc[...], ((1,), (1,)))
    count_row = exact_dot(ones, cnt[...], ((1,), (1,)))
    mine = jnp.where(tile_row == 2, loss_row, jnp.where(tile_row == 3, count_row, 0.0))
    lmine[...] = mine
    for block in range(1, 8):
        remote(lmine, lbuf.at[t], lsend, lrecv, peer(block)).start()
    lbuf[t] = mine

    remote(gbuf, gbuf, gsend, grecv, sibling).wait_recv()
    total = sbuf[O]
    for k in range(7):
        total = total + gbuf[k]
    remote(lbuf.at[pl.ds(0, 7)], lbuf.at[pl.ds(0, 7)], lsend, lrecv, sibling).wait_recv()
    group = lbuf[0]
    for k in range(1, 8):
        group = group + lbuf[k]
    for k in range(32):
        msg[k] = group
        msg[k, 0:2, :] = total[2 * k : 2 * k + 2, :]

    def scatter(step, carry):
        other, device = dp_peer(step)
        remote(msg.at[other], rbuf.at[d], msend, mrecv, device).start()
        return carry

    lax.fori_loop(1, 32, scatter, 0)
    rbuf[d] = msg[d]
    remote(rbuf.at[pl.ds(0, 31)], rbuf.at[pl.ds(0, 31)], msend, mrecv, sibling).wait_recv()
    whole = rbuf[0]
    for k in range(1, 32):
        whole = whole + rbuf[k]
    divisor = jnp.maximum(whole[3:4, :], 1.0)
    loss_o[...] = -whole[2:3, :] / divisor
    lane = lax.broadcasted_iota(jnp.int32, (2, 128), 1)
    row = lax.broadcasted_iota(jnp.int32, (2, 128), 0)
    own = jnp.sum(
        jnp.where(lane == 2 * d + row, jnp.broadcast_to(divisor, (2, 128)), 0.0),
        axis=1, keepdims=True,
    )
    grad_o[...] = -whole[0:2, :] / own

    x_copy.wait_send()
    remote(rx.at[pl.ds(0, 7)], rx.at[pl.ds(0, 7)], rsend, rrecv, sibling).wait_send()
    remote(wbuf, wbuf, wsend, xrecv, sibling).wait_send()
    remote(pbuf, pbuf, psend, xrecv, sibling).wait_send()
    remote(gbuf, gbuf, gsend, grecv, sibling).wait_send()
    remote(lbuf.at[pl.ds(0, 7)], lbuf.at[pl.ds(0, 7)], lsend, lrecv, sibling).wait_send()
    remote(rbuf.at[pl.ds(0, 31)], rbuf.at[pl.ds(0, 31)], msend, mrecv, sibling).wait_send()


def local_step(
    roll_x, queries, cache_k, cache_v, cache_len, tenant_roll, w_key, w_value, ia3_key,
    ia3_value, train_x, upstream, tenant_train, advantage,
):
    smem = pl.BlockSpec(memory_space=pltpu.SMEM)
    vmem = pl.BlockSpec(memory_space=pltpu.VMEM)
    anywhere = pl.BlockSpec(memory_space=pl.ANY)
    dma = pltpu.SemaphoreType.DMA
    attn_out, gradient, tenant_loss = pl.pallas_call(
        kernel,
        out_shape=(
            jax.ShapeDtypeStruct((16, 1024), BF16),
            jax.ShapeDtypeStruct((2, 128), F32),
            jax.ShapeDtypeStruct((1, 128), F32),
        ),
        in_specs=[smem, smem] + [anywhere] * 12,
        out_specs=(vmem, vmem, vmem),
        scratch_shapes=[
            pltpu.VMEM((7, HALF, HD), BF16),
            pltpu.VMEM((2 * HALF, HD), BF16),
            pltpu.VMEM((2 * HALF, HD), BF16),
            pltpu.VMEM((512, HALF), BF16),
            pltpu.VMEM((256, 1024), BF16),
            pltpu.VMEM((16, 256, HD), BF16),
            pltpu.VMEM((16, 256, HD), BF16),
            pltpu.VMEM((16, 1024), BF16),
            pltpu.VMEM((8, 16, 1024), BF16),
            pltpu.VMEM((TENANTS, HD), F32),
            pltpu.VMEM((TENANTS, 1024), F32),
            pltpu.VMEM((2, 128), jnp.int32),
            pltpu.VMEM((2, 128), jnp.int32),
            pltpu.VMEM((8, 512, HD), F32),
            pltpu.VMEM((8, 256, HD), F32),
            pltpu.VMEM((8, TENANTS, HD), F32),
            pltpu.VMEM((7, TENANTS, HD), F32),
            pltpu.VMEM((8, 128), F32),
            pltpu.VMEM((8, 8, 128), F32),
            pltpu.VMEM((32, 8, 128), F32),
            pltpu.VMEM((32, 8, 128), F32),
            pltpu.VMEM((128, HD), F32),
            pltpu.VMEM((128, 256), F32),
            pltpu.VMEM((128, HD), F32),
            pltpu.VMEM((128, 128), F32),
            pltpu.VMEM((TENANTS, 256), BF16),
            pltpu.VMEM((128, 128), F32),
            pltpu.VMEM((128, 128), F32),
            dma((12,)), dma, dma((4, 7)), dma((2, 7)), dma, dma, dma, dma, dma, dma((8,)),
            dma, dma, dma, dma, dma, dma,
        ],
        compiler_params=pltpu.CompilerParams(
            collective_id=0, has_side_effects=True, vmem_limit_bytes=60 * 1024 * 1024
        ),
    )(
        cache_len, tenant_roll, roll_x, queries, cache_k, cache_v, w_key, w_value, ia3_key,
        ia3_value, train_x, upstream, tenant_train.reshape(2, 128), advantage.reshape(2, 128),
    )
    return attn_out, gradient, tenant_loss[0, :TENANTS]


def solution(mesh):
    finer = Mesh(mesh.devices.reshape(2, 8, 2, 2, 4), AXES)
    placed = (
        P(DP, TENSOR), P(DP, TENSOR), P(DP, None, TENSOR), P(DP, None, TENSOR), P(DP), P(DP),
        P(None, TENSOR), P(None, TENSOR), P(), P(), P(DP_TENSOR, None), P(DP_TENSOR, None),
        P(DP_TENSOR), P(DP_TENSOR),
    )
    return jax.shard_map(
        local_step, mesh=finer, in_specs=placed, out_specs=(P(DP, TENSOR), P(DP, TENSOR), P()),
        check_vma=False,
    )
```

```python
import jax
import jax.numpy as jnp
from jax import lax
from jax.experimental import pallas as pl
from jax.experimental.pallas import tpu as pltpu
from jax.sharding import Mesh
from jax.sharding import PartitionSpec as P

HD = 128
TENANTS = 64
AXES = ("y_hi", "z", "core", "y_lo", "x")
DP = ("y_hi", "z", "core")
TENSOR = ("y_lo", "x")
DP_TENSOR = DP + TENSOR
MESH = pl.DeviceIdType.MESH
F32 = jnp.float32
BF16 = jnp.bfloat16

O, XM, XP, X2, F0, FM, FP, F2 = range(8)
SHIFT = ((0, 0), (0, 3), (0, 1), (0, 2), (1, 0), (1, 3), (1, 1), (1, 2))
INVERSE = (O, XP, XM, X2, F0, FP, FM, F2)

HALF = 4096
ZROWS = 1280
ZHALF = ZROWS // 2
QUARTER = ((0, 640), (640, 640), (1280, 768), (2048, 768))


def quarters(block, *which):
    return tuple((block, *QUARTER[k]) for k in which)


LINKS = (
    quarters(XM, 0, 1, 2, 3) + quarters(X2, 0, 2) + ((F2, 3072, 512), (F2, 3584, 512)),
    quarters(XP, 0, 1, 2, 3) + quarters(X2, 1, 3) + ((F2, 1024, 512), (F2, 2560, 512)),
    quarters(F0, 0, 2) + quarters(FM, 0, 1, 2, 3) + ((F2, 0, 512), (F2, 1536, 512)),
    quarters(F0, 1, 3) + quarters(FP, 0, 1, 2, 3) + ((F2, 512, 512), (F2, 2048, 512)),
)
ROUNDS = 8
SENT_AS = (
    {XM: O, X2: XM, F2: FM},
    {XP: O, X2: XP, F2: FP},
    {F0: O, FM: XM, FP: XP, F2: X2},
    {F0: O, FM: XM, FP: XP, F2: X2},
)
Z_SEND = {0: (F0,), 1: (XM, XP), 3: (FM, FP), 4: (X2,)}
Z_TAKE = {2: (F0,), 3: (XM,), 4: (XP, FM), 5: (FP,), 6: (X2,)}
FINISH = {1: (O,), 3: (F0,), 4: (XM,), 5: (XP,), 6: (FM, FP, X2), 7: (F2,)}
AFTER_Z = ((0, 6), (1, 7))


def dot(a, b):
    return jnp.dot(a, b, preferred_element_type=F32)


def exact_dot(a, b, dims):
    return lax.dot_general(
        a, b, (dims, ((), ())), precision=lax.Precision.HIGHEST, preferred_element_type=F32
    )


def kernel(
    clen, troll, roll_h, q_h, ck_h, cv_h, wk_h, wv_h, ik_h, iv_h, x_h, up_h, tt_h, adv_h,
    attn_o, whole_o,
    wbuf, wv, wk, xh, up, kc, vc, q, rx, ik, iv, tt, adv, tt2, adv2, acc, sbuf, gbuf, lmine, lbuf,
    msg, rbuf, qs, sc, mix, snew, mt, lacc, cnt,
    lsem, wsend, wrecv, zrecv, xsend, xrecv, rsend, rrecv, gsend, grecv,
    lsend, lrecv, msend, mrecv, known,
):
    y_hi, z, core, y_lo, x = (lax.axis_index(a) for a in AXES)
    d = y_hi * 16 + z * 2 + core
    t = y_lo * 4 + x
    odd = z % 2
    y = 2 * y_hi + y_lo
    y_up, y_down = (y + 1) % 4, (y + 3) % 4
    sibling = (y_hi, z, 1 - core, y_lo, x)
    z_up = (y_hi, (z + 1) % 8, core, y_lo, x)
    z_down = (y_hi, (z + 7) % 8, core, y_lo, x)
    to_link = (
        (y_hi, z, core, y_lo, (x + 1) % 4),
        (y_hi, z, core, y_lo, (x + 3) % 4),
        (y_up // 2, z, core, y_up % 2, x),
        (y_down // 2, z, core, y_down % 2, x),
    )

    def place(block):
        return (y_lo + SHIFT[block][0]) % 2, (x + SHIFT[block][1]) % 4

    def peer(block):
        py, px = place(block)
        return (y_hi, z, core, py, px)

    def columns(block):
        py, px = place(block)
        return pl.ds(pl.multiple_of((py * 4 + px) * HD, HD), HD)

    def dp_peer(step):
        other = (d + step) % 32
        return other, (other // 16, (other // 2) % 8, other % 2, y_lo, x)

    def remote(src, dst, send, recv, device):
        return pltpu.make_async_remote_copy(
            src_ref=src, dst_ref=dst, send_sem=send, recv_sem=recv,
            device_id=device, device_id_type=MESH,
        )

    own_half = pl.ds(pl.multiple_of(core * HALF, HALF), HALF)
    other_half = pl.ds(pl.multiple_of((1 - core) * HALF, HALF), HALF)
    local = [
        pltpu.make_async_copy(src, dst, lsem.at[k])
        for k, (src, dst) in enumerate(
            (
                (wv_h, wv),
                (x_h.at[:, own_half], xh.at[pl.ds(0, 256)]),
                (tt_h, tt),
                (adv_h, adv),
                (up_h, up.at[pl.ds(0, 256)]),
                (wk_h, wk),
                (roll_h, rx.at[t]),
                (ik_h.at[:, pl.ds(pl.multiple_of(t * HD, HD), HD)], ik),
                (iv_h, iv),
                (q_h, q),
                (ck_h, kc),
                (cv_h, vc),
            )
        )
    ]
    for copy in local:
        copy.start()

    barrier = pltpu.get_barrier_semaphore()
    neighbours = to_link + (z_up, z_down, sibling)

    def tell(semaphore):
        for device in neighbours:
            pl.semaphore_signal(semaphore, inc=1, device_id=device, device_id_type=MESH)

    def hear(semaphore):
        pl.semaphore_wait(semaphore, len(neighbours))

    tell(barrier)
    hear(barrier)

    def rows(first, length):
        return pl.multiple_of((1 - odd) * first + odd * (HALF - first - length), 128)

    def link_copy(link, r):
        block, first, length = LINKS[link][r]
        source = SENT_AS[link][block]
        row = rows(first, length)
        if source == O:
            src = wv_h.at[pl.ds(pl.multiple_of(core * HALF + row, 128), length)]
        else:
            src = wbuf.at[source - 1, pl.ds(row, length)]
        return remote(
            src, wbuf.at[block - 1, pl.ds(row, length)], wsend, wrecv.at[link, r], to_link[link]
        )

    def z_copy(block, h, base):
        ref = wbuf.at[block - 1, pl.ds(pl.multiple_of(base + h * ZHALF, 128), ZHALF)]
        return remote(ref, ref, wsend, zrecv.at[h, block - 1], z_up if h == 0 else z_down)

    z_sent = odd * (HALF - ZROWS)
    z_taken = (1 - odd) * (HALF - ZROWS)

    def issue(r):
        for link in range(4):
            if (link, r) not in AFTER_Z:
                link_copy(link, r).start()

    issue(0)
    issue(1)
    tell(known.at[0])
    exchange = [
        remote(src, dst, xsend.at[k], xrecv.at[k], sibling)
        for k, (src, dst) in enumerate(
            (
                (x_h.at[:, other_half], xh.at[pl.ds(256, 256)]),
                (up_h, up.at[pl.ds(256, 256)]),
                (tt_h, tt2),
                (adv_h, adv2),
            )
        )
    ]
    for copy in exchange:
        copy.start()
    roll_sends = [
        remote(roll_h, rx.at[t], rsend, rrecv, peer(block)) for block in range(1, 8)
    ]

    def product(block, row, length, first=False):
        if block == O:
            part = wv[pl.ds(pl.multiple_of(core * HALF + row, 128), length), :]
        else:
            part = wbuf[block - 1, pl.ds(row, length), :]
        new = dot(xh[:, pl.ds(pl.multiple_of(row, 128), length)], part)
        if first:
            acc[block] = new
        else:
            acc[block] += new

    def sum_copy(block):
        return remote(
            sbuf.at[block], gbuf.at[INVERSE[block] - 1], gsend, grecv, peer(block)
        )

    def finish(block, first=False):
        weighted = acc[block] * up[:, columns(block)].astype(F32)
        high = weighted.astype(BF16)
        low = (weighted - high.astype(F32)).astype(BF16)
        sums = dot(mt[...], high) + dot(mt[...], low)
        sbuf[block] = sums
        if block != O:
            sum_copy(block).start()
        part = sums * iv[:, columns(block)]
        if first:
            lacc[0:64, :] = part
        else:
            lacc[0:64, :] += part

    for k in (2, 3):
        local[k].wait()
    hear(known.at[0])
    tell(known.at[1])
    for k in (2, 3):
        exchange[k].wait_recv()
    tenant = lax.broadcasted_iota(jnp.int32, (64, 128), 0)
    hits = []
    for k in range(4):
        labels, gains = (tt, adv) if k < 2 else (tt2, adv2)
        k2 = k % 2
        hits.append(
            (tenant == jnp.broadcast_to(labels[k2 : k2 + 1, :], (64, 128))).astype(F32)
        )
        gain = jnp.broadcast_to(gains[k2 : k2 + 1, :].astype(F32), (64, 128))
        mt[:, k * 128 : (k + 1) * 128] = (hits[k] * gain).astype(BF16)
    cnt[0:64, :] = hits[0] + hits[1]
    cnt[64:128, :] = jnp.zeros((64, 128), F32)
    lacc[64:128, :] = jnp.zeros((64, 128), F32)

    scale = 1.0 / jnp.sqrt(F32(HD))

    def spread(h, transposed=False):
        shape = (16, 128) if transposed else (128, 16)
        pair = lax.broadcasted_iota(jnp.int32, shape, 1 if transposed else 0)
        row = lax.broadcasted_iota(jnp.int32, shape, 0 if transposed else 1)
        if h is None:
            return (pair // 8 == row).astype(F32).astype(BF16)
        return (pair == row * 8 + h).astype(F32).astype(BF16)

    def project():
        for k in (5, 6, 7, 9):
            local[k].wait()
        remote(rx.at[pl.ds(0, 7)], rx.at[pl.ds(0, 7)], rsend, rrecv, sibling).wait_recv()
        key_sum = jnp.zeros((16, HD), F32)
        value_sum = jnp.zeros((16, HD), F32)
        for k in range(8):
            part = rx[k]
            key_sum = key_sum + dot(part, wk[k * 1024 : (k + 1) * 1024, :])
            value_sum = value_sum + dot(part, wv[k * 1024 : (k + 1) * 1024, :])
        row = lax.broadcasted_iota(jnp.int32, (16, TENANTS), 0)
        owner = jnp.zeros((16, TENANTS), jnp.int32)
        for r in range(16):
            owner = jnp.where(row == r, troll[r], owner)
        onehot = (owner == lax.broadcasted_iota(jnp.int32, (16, TENANTS), 1)).astype(F32)
        key_gain = exact_dot(onehot, ik[...], ((1,), (0,)))
        value_gain = exact_dot(onehot, iv[:, columns(O)], ((1,), (0,)))
        key_new = (key_sum * key_gain).astype(BF16)
        value_new = (value_sum * value_gain).astype(BF16)
        queries = jnp.zeros((128, HD), F32)
        for h in range(8):
            queries = queries + dot(spread(h), q[:, h * HD : (h + 1) * HD])
        qs[...] = queries
        each = spread(None)
        snew[...] = jnp.broadcast_to(
            jnp.sum(queries * dot(each, key_new), axis=1, keepdims=True) * scale, (128, 128)
        )
        mix[...] = dot(each, value_new)

    def score():
        local[10].wait()
        place_in_cache = lax.broadcasted_iota(jnp.int32, (8, 256), 1)
        for r in range(16):
            s = lax.dot_general(
                qs[r * 8 : (r + 1) * 8, :].astype(BF16), kc[r], (((1,), (1,)), ((), ())),
                preferred_element_type=F32,
            ) * scale
            sc[r * 8 : (r + 1) * 8, :] = jnp.where(place_in_cache < clen[r], s, -jnp.inf)

    def normalise():
        s = sc[...]
        new = snew[:, 0:1]
        highest = jnp.maximum(jnp.max(s, axis=1, keepdims=True), new)
        expo = jnp.exp(s - highest)
        expo_new = jnp.exp(new - highest)
        denominator = jnp.sum(expo, axis=1, keepdims=True) + expo_new
        sc[...] = (expo / denominator).astype(BF16).astype(F32)
        mix[...] = (expo_new / denominator).astype(BF16).astype(F32) * mix[...]

    def mixture():
        local[11].wait()
        for r in range(16):
            rows = slice(r * 8, (r + 1) * 8)
            mix[rows, :] += dot(sc[rows, :].astype(BF16), vc[r])
        mixed = mix[...].astype(BF16)
        for h in range(8):
            attn_o[:, h * HD : (h + 1) * HD] = dot(spread(h, True), mixed).astype(BF16)

    beside = {2: project, 3: score, 4: normalise, 5: mixture}

    hear(known.at[1])
    for copy in roll_sends:
        copy.start()
    tell(known.at[2])
    for k in (0, 1, 4, 8):
        local[k].wait()
    exchange[0].wait_recv()
    for k in range(4):
        product(O, k * 1024, 1024, k == 0)
    exchange[1].wait_recv()

    seen = {O}
    for r in range(ROUNDS):
        for link in range(4):
            link_copy(link, r).wait_recv()
        if r + 2 < ROUNDS:
            issue(r + 2)
        for block in Z_SEND.get(r, ()):
            for h in range(2):
                z_copy(block, h, z_sent).start()
        if r < 4:
            hear(known.at[r + 2])
            if r < 3:
                tell(known.at[r + 3])
        for link in range(4):
            block, first, length = LINKS[link][r]
            product(block, rows(first, length), length, block not in seen)
            seen.add(block)
        for block in Z_TAKE.get(r, ()):
            for h in range(2):
                z_copy(block, h, z_taken).wait_recv()
        for link, later in AFTER_Z:
            if later == r + 2:
                link_copy(link, later).start()
        for block in Z_TAKE.get(r, ()):
            product(block, pl.multiple_of(z_taken, 128), ZROWS)
        if r in beside:
            beside[r]()
        for block in FINISH.get(r, ()):
            finish(block, block == O)

    ones = jnp.ones((8, 128), F32)
    tile_row = lax.broadcasted_iota(jnp.int32, (8, 128), 0)
    loss_row = exact_dot(ones, lacc[...], ((1,), (1,)))
    count_row = exact_dot(ones, cnt[...], ((1,), (1,)))
    mine = jnp.where(tile_row == 2, loss_row, jnp.where(tile_row == 3, count_row, 0.0))
    lmine[...] = mine
    for block in range(1, 8):
        remote(lmine, lbuf.at[t], lsend, lrecv, peer(block)).start()
    lbuf[t] = mine

    remote(gbuf, gbuf, gsend, grecv, sibling).wait_recv()
    total = sbuf[O]
    for k in range(7):
        total = total + gbuf[k]
    remote(lbuf.at[pl.ds(0, 7)], lbuf.at[pl.ds(0, 7)], lsend, lrecv, sibling).wait_recv()
    group = lbuf[0]
    for k in range(1, 8):
        group = group + lbuf[k]
    for k in range(32):
        msg[k] = group
        msg[k, 0:2, :] = total[2 * k : 2 * k + 2, :]

    def scatter(step, carry):
        other, device = dp_peer(step)
        remote(msg.at[other], rbuf.at[d], msend, mrecv, device).start()
        return carry

    lax.fori_loop(1, 32, scatter, 0)
    rbuf[d] = msg[d]
    remote(rbuf.at[pl.ds(0, 31)], rbuf.at[pl.ds(0, 31)], msend, mrecv, sibling).wait_recv()
    whole = rbuf[0]
    for k in range(1, 32):
        whole = whole + rbuf[k]
    whole_o[...] = whole

    for copy in exchange:
        copy.wait_send()
    remote(rx.at[pl.ds(0, 7)], rx.at[pl.ds(0, 7)], rsend, rrecv, sibling).wait_send()
    remote(wbuf, wbuf, wsend, grecv, sibling).wait_send()
    remote(gbuf, gbuf, gsend, grecv, sibling).wait_send()
    remote(lbuf.at[pl.ds(0, 7)], lbuf.at[pl.ds(0, 7)], lsend, lrecv, sibling).wait_send()
    remote(rbuf.at[pl.ds(0, 31)], rbuf.at[pl.ds(0, 31)], msend, mrecv, sibling).wait_send()


def outputs(attn, whole, attn_o, grad_o, loss_o):
    d = lax.axis_index("y_hi") * 16 + lax.axis_index("z") * 2 + lax.axis_index("core")
    attn_o[...] = attn[...]
    divisor = jnp.maximum(whole[3:4, :], 1.0)
    loss_o[...] = (-whole[2:3, :] / divisor)[:, 0:TENANTS]
    lane = lax.broadcasted_iota(jnp.int32, (2, 128), 1)
    row = lax.broadcasted_iota(jnp.int32, (2, 128), 0)
    own = jnp.sum(
        jnp.where(lane == 2 * d + row, jnp.broadcast_to(divisor, (2, 128)), 0.0),
        axis=1, keepdims=True,
    )
    grad_o[...] = -whole[0:2, :] / own


def local_step(
    roll_x, queries, cache_k, cache_v, cache_len, tenant_roll, w_key, w_value, ia3_key,
    ia3_value, train_x, upstream, tenant_train, advantage,
):
    smem = pl.BlockSpec(memory_space=pltpu.SMEM)
    vmem = pl.BlockSpec(memory_space=pltpu.VMEM)
    anywhere = pl.BlockSpec(memory_space=pl.ANY)
    dma = pltpu.SemaphoreType.DMA
    attn, whole = pl.pallas_call(
        kernel,
        out_shape=(
            jax.ShapeDtypeStruct((16, 1024), BF16),
            jax.ShapeDtypeStruct((8, 128), F32),
        ),
        in_specs=[smem, smem] + [anywhere] * 12,
        out_specs=(vmem, vmem),
        scratch_shapes=[
            pltpu.VMEM((7, HALF, HD), BF16),
            pltpu.VMEM((2 * HALF, HD), BF16),
            pltpu.VMEM((2 * HALF, HD), BF16),
            pltpu.VMEM((512, HALF), BF16),
            pltpu.VMEM((512, 1024), BF16),
            pltpu.VMEM((16, 256, HD), BF16),
            pltpu.VMEM((16, 256, HD), BF16),
            pltpu.VMEM((16, 1024), BF16),
            pltpu.VMEM((8, 16, 1024), BF16),
            pltpu.VMEM((TENANTS, HD), F32),
            pltpu.VMEM((TENANTS, 1024), F32),
            pltpu.VMEM((2, 128), jnp.int32),
            pltpu.VMEM((2, 128), jnp.int32),
            pltpu.VMEM((2, 128), jnp.int32),
            pltpu.VMEM((2, 128), jnp.int32),
            pltpu.VMEM((8, 512, HD), F32),
            pltpu.VMEM((8, TENANTS, HD), F32),
            pltpu.VMEM((7, TENANTS, HD), F32),
            pltpu.VMEM((8, 128), F32),
            pltpu.VMEM((8, 8, 128), F32),
            pltpu.VMEM((32, 8, 128), F32),
            pltpu.VMEM((32, 8, 128), F32),
            pltpu.VMEM((128, HD), F32),
            pltpu.VMEM((128, 256), F32),
            pltpu.VMEM((128, HD), F32),
            pltpu.VMEM((128, 128), F32),
            pltpu.VMEM((TENANTS, 512), BF16),
            pltpu.VMEM((128, 128), F32),
            pltpu.VMEM((128, 128), F32),
            dma((12,)), dma, dma((4, ROUNDS)), dma((2, 7)), dma((4,)), dma((4,)), dma, dma,
            dma, dma, dma, dma, dma, dma, pltpu.SemaphoreType.REGULAR((6,)),
        ],
        compiler_params=pltpu.CompilerParams(
            collective_id=0, has_side_effects=True, vmem_limit_bytes=60 * 1024 * 1024
        ),
    )(
        cache_len, tenant_roll, roll_x, queries, cache_k, cache_v, w_key, w_value, ia3_key,
        ia3_value, train_x, upstream, tenant_train.reshape(2, 128), advantage.reshape(2, 128),
    )
    attn_out, gradient, tenant_loss = pl.pallas_call(
        outputs,
        out_shape=(
            jax.ShapeDtypeStruct((16, 1024), BF16),
            jax.ShapeDtypeStruct((2, 128), F32),
            jax.ShapeDtypeStruct((1, TENANTS), F32),
        ),
        in_specs=[vmem, vmem],
        out_specs=(vmem, vmem, vmem),
    )(attn, whole)
    return attn_out, gradient, tenant_loss.reshape(TENANTS)


def solution(mesh):
    finer = Mesh(mesh.devices.reshape(2, 8, 2, 2, 4), AXES)
    placed = (
        P(DP, TENSOR), P(DP, TENSOR), P(DP, None, TENSOR), P(DP, None, TENSOR), P(DP), P(DP),
        P(None, TENSOR), P(None, TENSOR), P(), P(), P(DP_TENSOR, None), P(DP_TENSOR, None),
        P(DP_TENSOR), P(DP_TENSOR),
    )
    return jax.shard_map(
        local_step, mesh=finer, in_specs=placed, out_specs=(P(DP, TENSOR), P(DP, TENSOR), P()),
        check_vma=False,
    )
```

```python
import jax
import jax.numpy as jnp
from jax import lax
from jax.experimental import pallas as pl
from jax.experimental.pallas import tpu as pltpu
from jax.sharding import Mesh
from jax.sharding import PartitionSpec as P

HD = 128
TENANTS = 64
AXES = ("y_hi", "z", "core", "y_lo", "x")
DP = ("y_hi", "z", "core")
TENSOR = ("y_lo", "x")
DP_TENSOR = DP + TENSOR
MESH = pl.DeviceIdType.MESH
F32 = jnp.float32
BF16 = jnp.bfloat16

O, XM, XP, X2, F0, FM, FP, F2 = range(8)
SHIFT = ((0, 0), (0, 3), (0, 1), (0, 2), (1, 0), (1, 3), (1, 1), (1, 2))
INVERSE = (O, XP, XM, X2, F0, FP, FM, F2)

HALF = 4096
ZROWS = 1280
ZHALF = ZROWS // 2
QUARTER = ((0, 640), (640, 640), (1280, 768), (2048, 768))


def quarters(block, *which):
    return tuple((block, *QUARTER[k]) for k in which)


LINKS = (
    quarters(XM, 0, 1, 2, 3) + quarters(X2, 0, 2) + ((F2, 3072, 512), (F2, 3584, 512)),
    quarters(XP, 0, 1, 2, 3) + quarters(X2, 1, 3) + ((F2, 1024, 512), (F2, 2560, 512)),
    quarters(F0, 0, 2) + quarters(FM, 0, 1, 2, 3) + ((F2, 0, 512), (F2, 1536, 512)),
    quarters(F0, 1, 3) + quarters(FP, 0, 1, 2, 3) + ((F2, 512, 512), (F2, 2048, 512)),
)
ROUNDS = 8
SENT_AS = (
    {XM: O, X2: XM, F2: FM},
    {XP: O, X2: XP, F2: FP},
    {F0: O, FM: XM, FP: XP, F2: X2},
    {F0: O, FM: XM, FP: XP, F2: X2},
)
Z_SEND = {0: (F0,), 1: (XM, XP), 3: (FM, FP), 4: (X2,)}
Z_TAKE = {2: (F0,), 4: (XM, XP, FM), 5: (FP,), 6: (X2,)}
PRODUCTS = {
    1: (((O, F0), 0, 1280), ((XM, XP), 0, 640), ((O, F0), 1280, 1536), ((XM, XP), 640, 640)),
    2: (((XM, XP), 1280, 768), ((FM, FP), 0, 640), ((O, F0), 2816, 1280)),
    3: (((XM, XP), 2048, 768), ((FM, FP), 640, 640)),
    4: (((X2,), 0, 1280), ((FM, FP), 1280, 768), ((XM, XP), 2816, 1280)),
    5: (((X2,), 1280, 1536), ((FM, FP), 2048, 768), ((FM, FP), 2816, 1280)),
    6: (((F2,), 0, 1536), ((F2,), 3072, 512), ((X2,), 2816, 1280)),
    7: (((F2,), 1536, 1536), ((F2,), 3584, 512)),
}
FINISH = {3: (O, F0), 4: (XM,), 5: (XP,), 6: (FM, FP, X2), 7: (F2,)}
AFTER_Z = ((0, 6), (1, 7))


def dot(a, b):
    return jnp.dot(a, b, preferred_element_type=F32)


def exact_dot(a, b, dims):
    return lax.dot_general(
        a, b, (dims, ((), ())), precision=lax.Precision.HIGHEST, preferred_element_type=F32
    )


def kernel(
    clen, troll, roll_h, q_h, ck_h, cv_h, wk_h, wv_h, ik_h, iv_h, x_h, up_h, tt_h, adv_h,
    attn_o, whole_o,
    wbuf, wv, wk, xh, up, kc, vc, q, rx, ik, iv, tt, adv, tt2, adv2, acc, sbuf, gbuf, lmine, lbuf,
    msg, rbuf, qs, sc, mix, snew, mt, lacc, cnt,
    lsem, wsend, wrecv, zrecv, xsend, xrecv, rsend, rrecv, gsend, grecv,
    lsend, lrecv, msend, mrecv, known,
):
    y_hi, z, core, y_lo, x = (lax.axis_index(a) for a in AXES)
    t = y_lo * 4 + x
    odd = z % 2
    y = 2 * y_hi + y_lo
    y_up, y_down = (y + 1) % 4, (y + 3) % 4
    sibling = (y_hi, z, 1 - core, y_lo, x)
    z_up = (y_hi, (z + 1) % 8, core, y_lo, x)
    z_down = (y_hi, (z + 7) % 8, core, y_lo, x)
    to_link = (
        (y_hi, z, core, y_lo, (x + 1) % 4),
        (y_hi, z, core, y_lo, (x + 3) % 4),
        (y_up // 2, z, core, y_up % 2, x),
        (y_down // 2, z, core, y_down % 2, x),
    )

    def place(block):
        return (y_lo + SHIFT[block][0]) % 2, (x + SHIFT[block][1]) % 4

    def peer(block):
        py, px = place(block)
        return (y_hi, z, core, py, px)

    def columns(block):
        py, px = place(block)
        return pl.ds(pl.multiple_of((py * 4 + px) * HD, HD), HD)

    def plane_peer(step):
        other = (y * 4 + x + step) % 16
        return other, (other // 8, z, core, (other // 4) % 2, other % 4)

    def column_peer(step):
        other = (z * 2 + core + step) % 16
        return other, (y_hi, other // 2, other % 2, y_lo, x)

    def remote(src, dst, send, recv, device):
        return pltpu.make_async_remote_copy(
            src_ref=src, dst_ref=dst, send_sem=send, recv_sem=recv,
            device_id=device, device_id_type=MESH,
        )

    own_half = pl.ds(pl.multiple_of(core * HALF, HALF), HALF)
    other_half = pl.ds(pl.multiple_of((1 - core) * HALF, HALF), HALF)
    local = [
        pltpu.make_async_copy(src, dst, lsem.at[k])
        for k, (src, dst) in enumerate(
            (
                (wv_h, wv),
                (x_h.at[:, own_half], xh.at[pl.ds(0, 256)]),
                (tt_h, tt),
                (adv_h, adv),
                (up_h, up.at[pl.ds(0, 256)]),
                (wk_h, wk),
                (roll_h, rx.at[t]),
                (ik_h.at[:, pl.ds(pl.multiple_of(t * HD, HD), HD)], ik),
                (iv_h, iv),
                (q_h, q),
                (ck_h, kc),
                (cv_h, vc),
            )
        )
    ]
    for copy in local:
        copy.start()

    barrier = pltpu.get_barrier_semaphore()
    neighbours = to_link + (z_up, z_down, sibling)

    def tell(semaphore):
        for device in neighbours:
            pl.semaphore_signal(semaphore, inc=1, device_id=device, device_id_type=MESH)

    def hear(semaphore):
        pl.semaphore_wait(semaphore, len(neighbours))

    tell(barrier)
    hear(barrier)

    def rows(first, length):
        return pl.multiple_of((1 - odd) * first + odd * (HALF - first - length), 128)

    def link_copy(link, r):
        block, first, length = LINKS[link][r]
        source = SENT_AS[link][block]
        row = rows(first, length)
        if source == O:
            src = wv_h.at[pl.ds(pl.multiple_of(core * HALF + row, 128), length)]
        else:
            src = wbuf.at[source - 1, pl.ds(row, length)]
        return remote(
            src, wbuf.at[block - 1, pl.ds(row, length)], wsend, wrecv.at[link, r], to_link[link]
        )

    def z_copy(block, h, base):
        ref = wbuf.at[block - 1, pl.ds(pl.multiple_of(base + h * ZHALF, 128), ZHALF)]
        return remote(ref, ref, wsend, zrecv.at[h, block - 1], z_up if h == 0 else z_down)

    z_sent = odd * (HALF - ZROWS)
    z_taken = (1 - odd) * (HALF - ZROWS)

    def issue(r):
        for link in range(4):
            if (link, r) not in AFTER_Z:
                link_copy(link, r).start()

    issue(0)
    issue(1)
    tell(known.at[0])
    exchange = [
        remote(src, dst, xsend.at[k], xrecv.at[k], sibling)
        for k, (src, dst) in enumerate(
            (
                (x_h.at[:, other_half], xh.at[pl.ds(256, 256)]),
                (up_h, up.at[pl.ds(256, 256)]),
                (tt_h, tt2),
                (adv_h, adv2),
            )
        )
    ]
    for copy in exchange:
        copy.start()
    roll_sends = [
        remote(roll_h, rx.at[t], rsend, rrecv, peer(block)) for block in range(1, 8)
    ]

    def part_of(block, row, length):
        if block == O:
            return wv[pl.ds(pl.multiple_of(core * HALF + row, 128), length), :]
        return wbuf[block - 1, pl.ds(row, length), :]

    def product(blocks, first, length, new):
        row = rows(first, length)
        parts = [part_of(block, row, length) for block in blocks]
        both = parts[0] if len(parts) == 1 else jnp.concatenate(parts, axis=1)
        result = dot(xh[:, pl.ds(row, length)], both)
        for k, block in enumerate(blocks):
            if new:
                acc[block] = result[:, k * HD : (k + 1) * HD]
            else:
                acc[block] += result[:, k * HD : (k + 1) * HD]

    def sum_copies(block):
        copies = []
        for k, high in enumerate((y_hi, 1 - y_hi)):
            slot = INVERSE[block] + 8 * k
            if slot > 0:
                py, px = place(block)
                copies.append(
                    remote(
                        sbuf.at[block, pl.ds(pl.multiple_of(32 * high, 32), 32)],
                        gbuf.at[slot - 1], gsend, grecv, (high, z, core, py, px),
                    )
                )
        return copies

    def finish(block, first=False):
        weighted = acc[block] * up[:, columns(block)].astype(F32)
        high = weighted.astype(BF16)
        low = (weighted - high.astype(F32)).astype(BF16)
        sums = dot(mt[...], high) + dot(mt[...], low)
        sbuf[block] = sums
        for copy in sum_copies(block):
            copy.start()
        part = sums * iv[:, columns(block)]
        if first:
            lacc[0:64, :] = part
        else:
            lacc[0:64, :] += part

    def table():
        for k in (2, 3):
            local[k].wait()
        for k in (2, 3):
            exchange[k].wait_recv()
        tenant = lax.broadcasted_iota(jnp.int32, (64, 128), 0)
        hits = []
        for k in range(4):
            labels, gains = (tt, adv) if k < 2 else (tt2, adv2)
            k2 = k % 2
            hits.append(
                (tenant == jnp.broadcast_to(labels[k2 : k2 + 1, :], (64, 128))).astype(F32)
            )
            gain = jnp.broadcast_to(gains[k2 : k2 + 1, :].astype(F32), (64, 128))
            mt[:, k * 128 : (k + 1) * 128] = (hits[k] * gain).astype(BF16)
        cnt[0:64, :] = hits[0] + hits[1]
        cnt[64:128, :] = jnp.zeros((64, 128), F32)
        lacc[64:128, :] = jnp.zeros((64, 128), F32)

    scale = 1.0 / jnp.sqrt(F32(HD))

    def spread(h, transposed=False):
        shape = (16, 128) if transposed else (128, 16)
        pair = lax.broadcasted_iota(jnp.int32, shape, 1 if transposed else 0)
        row = lax.broadcasted_iota(jnp.int32, shape, 0 if transposed else 1)
        if h is None:
            return (pair // 8 == row).astype(F32).astype(BF16)
        return (pair == row * 8 + h).astype(F32).astype(BF16)

    def project():
        for k in (5, 6, 7, 9):
            local[k].wait()
        remote(rx.at[pl.ds(0, 7)], rx.at[pl.ds(0, 7)], rsend, rrecv, sibling).wait_recv()
        key_sum = jnp.zeros((16, HD), F32)
        value_sum = jnp.zeros((16, HD), F32)
        for k in range(8):
            part = rx[k]
            key_sum = key_sum + dot(part, wk[k * 1024 : (k + 1) * 1024, :])
            value_sum = value_sum + dot(part, wv[k * 1024 : (k + 1) * 1024, :])
        row = lax.broadcasted_iota(jnp.int32, (16, TENANTS), 0)
        owner = jnp.zeros((16, TENANTS), jnp.int32)
        for r in range(16):
            owner = jnp.where(row == r, troll[r], owner)
        onehot = (owner == lax.broadcasted_iota(jnp.int32, (16, TENANTS), 1)).astype(F32)
        key_gain = exact_dot(onehot, ik[...], ((1,), (0,)))
        value_gain = exact_dot(onehot, iv[:, columns(O)], ((1,), (0,)))
        key_new = (key_sum * key_gain).astype(BF16)
        value_new = (value_sum * value_gain).astype(BF16)
        queries = jnp.zeros((128, HD), F32)
        for h in range(8):
            queries = queries + dot(spread(h), q[:, h * HD : (h + 1) * HD])
        qs[...] = queries
        each = spread(None)
        snew[...] = jnp.broadcast_to(
            jnp.sum(queries * dot(each, key_new), axis=1, keepdims=True) * scale, (128, 128)
        )
        mix[...] = dot(each, value_new)

    def score():
        local[10].wait()
        place_in_cache = lax.broadcasted_iota(jnp.int32, (8, 256), 1)
        for r in range(16):
            s = lax.dot_general(
                qs[r * 8 : (r + 1) * 8, :].astype(BF16), kc[r], (((1,), (1,)), ((), ())),
                preferred_element_type=F32,
            ) * scale
            sc[r * 8 : (r + 1) * 8, :] = jnp.where(place_in_cache < clen[r], s, -jnp.inf)

    def normalise():
        s = sc[...]
        new = snew[:, 0:1]
        highest = jnp.maximum(jnp.max(s, axis=1, keepdims=True), new)
        expo = jnp.exp(s - highest)
        expo_new = jnp.exp(new - highest)
        denominator = jnp.sum(expo, axis=1, keepdims=True) + expo_new
        sc[...] = (expo / denominator).astype(BF16).astype(F32)
        mix[...] = (expo_new / denominator).astype(BF16).astype(F32) * mix[...]

    def mixture():
        local[11].wait()
        for r in range(16):
            rows = slice(r * 8, (r + 1) * 8)
            mix[rows, :] += dot(sc[rows, :].astype(BF16), vc[r])
        mixed = mix[...].astype(BF16)
        for h in range(8):
            attn_o[:, h * HD : (h + 1) * HD] = dot(spread(h, True), mixed).astype(BF16)

    ones = jnp.ones((8, 128), F32)
    tile_row = lax.broadcasted_iota(jnp.int32, (8, 128), 0)

    def loss_and_count():
        loss_row = exact_dot(ones, lacc[...], ((1,), (1,)))
        count_row = exact_dot(ones, cnt[...], ((1,), (1,)))
        return jnp.where(tile_row == 2, loss_row, jnp.where(tile_row == 3, count_row, 0.0))

    beside = {2: project, 3: score, 4: normalise, 5: mixture}

    hear(known.at[0])
    tell(known.at[1])
    seen = set()
    for r in range(ROUNDS):
        for link in range(4):
            link_copy(link, r).wait_recv()
        if r + 2 < ROUNDS:
            issue(r + 2)
        for block in Z_SEND.get(r, ()):
            for h in range(2):
                z_copy(block, h, z_sent).start()
        if r < 3:
            hear(known.at[r + 1])
            if r < 2:
                tell(known.at[r + 2])
        if r == 0:
            for copy in roll_sends:
                copy.start()
            table()
            for k in (0, 1, 4, 8):
                local[k].wait()
        if r == 1:
            exchange[0].wait_recv()
            exchange[1].wait_recv()
        for block in Z_TAKE.get(r, ()):
            for h in range(2):
                z_copy(block, h, z_taken).wait_recv()
        for link, later in AFTER_Z:
            if later == r + 2:
                link_copy(link, later).start()
        for blocks, first, length in PRODUCTS.get(r, ()):
            product(blocks, first, length, blocks[0] not in seen)
            seen.update(blocks)
        if r in beside:
            beside[r]()
        for block in FINISH.get(r, ()):
            finish(block, block in (O, F2))
        if r == ROUNDS - 2:
            lmine[...] = loss_and_count()

    group = y * 4 + x
    mine = lmine[...] + jnp.where(tile_row == 2, exact_dot(ones, lacc[...], ((1,), (1,))), 0.0)
    lmine[...] = mine
    for step in range(1, 16):
        remote(lmine, lbuf.at[group], lsend, lrecv, plane_peer(step)[1]).start()
    lbuf[group] = mine

    remote(gbuf, gbuf, gsend, grecv, sibling).wait_recv()
    total = sbuf[O, pl.ds(pl.multiple_of(32 * y_hi, 32), 32), :]
    for k in range(15):
        total = total + gbuf[k]
    remote(lbuf.at[pl.ds(0, 15)], lbuf.at[pl.ds(0, 15)], lsend, lrecv, sibling).wait_recv()
    plane = lbuf[0]
    for k in range(1, 16):
        plane = plane + lbuf[k]
    for k in range(16):
        msg[k] = plane
        msg[k, 0:2, :] = total[2 * k : 2 * k + 2, :]
    own = z * 2 + core
    for step in range(1, 16):
        other, device = column_peer(step)
        remote(msg.at[other], rbuf.at[own], msend, mrecv, device).start()
    rbuf[own] = msg[own]
    remote(rbuf.at[pl.ds(0, 15)], rbuf.at[pl.ds(0, 15)], msend, mrecv, sibling).wait_recv()
    whole = rbuf[0]
    for k in range(1, 16):
        whole = whole + rbuf[k]
    whole_o[...] = whole

    for copy in exchange:
        copy.wait_send()
    remote(rx.at[pl.ds(0, 7)], rx.at[pl.ds(0, 7)], rsend, rrecv, sibling).wait_send()
    remote(wbuf, wbuf, wsend, grecv, sibling).wait_send()
    remote(gbuf, gbuf, gsend, grecv, sibling).wait_send()
    remote(lbuf.at[pl.ds(0, 15)], lbuf.at[pl.ds(0, 15)], lsend, lrecv, sibling).wait_send()
    remote(rbuf.at[pl.ds(0, 15)], rbuf.at[pl.ds(0, 15)], msend, mrecv, sibling).wait_send()


def outputs(attn, whole, attn_o, grad_o, loss_o):
    d = lax.axis_index("y_hi") * 16 + lax.axis_index("z") * 2 + lax.axis_index("core")
    attn_o[...] = attn[...]
    divisor = jnp.maximum(whole[3:4, :], 1.0)
    loss_o[...] = (-whole[2:3, :] / divisor)[:, 0:TENANTS]
    lane = lax.broadcasted_iota(jnp.int32, (2, 128), 1)
    row = lax.broadcasted_iota(jnp.int32, (2, 128), 0)
    own = jnp.sum(
        jnp.where(lane == 2 * d + row, jnp.broadcast_to(divisor, (2, 128)), 0.0),
        axis=1, keepdims=True,
    )
    grad_o[...] = -whole[0:2, :] / own


def local_step(
    roll_x, queries, cache_k, cache_v, cache_len, tenant_roll, w_key, w_value, ia3_key,
    ia3_value, train_x, upstream, tenant_train, advantage,
):
    smem = pl.BlockSpec(memory_space=pltpu.SMEM)
    vmem = pl.BlockSpec(memory_space=pltpu.VMEM)
    anywhere = pl.BlockSpec(memory_space=pl.ANY)
    dma = pltpu.SemaphoreType.DMA
    attn, whole = pl.pallas_call(
        kernel,
        out_shape=(
            jax.ShapeDtypeStruct((16, 1024), BF16),
            jax.ShapeDtypeStruct((8, 128), F32),
        ),
        in_specs=[smem, smem] + [anywhere] * 12,
        out_specs=(vmem, vmem),
        scratch_shapes=[
            pltpu.VMEM((7, HALF, HD), BF16),
            pltpu.VMEM((2 * HALF, HD), BF16),
            pltpu.VMEM((2 * HALF, HD), BF16),
            pltpu.VMEM((512, HALF), BF16),
            pltpu.VMEM((512, 1024), BF16),
            pltpu.VMEM((16, 256, HD), BF16),
            pltpu.VMEM((16, 256, HD), BF16),
            pltpu.VMEM((16, 1024), BF16),
            pltpu.VMEM((8, 16, 1024), BF16),
            pltpu.VMEM((TENANTS, HD), F32),
            pltpu.VMEM((TENANTS, 1024), F32),
            pltpu.VMEM((2, 128), jnp.int32),
            pltpu.VMEM((2, 128), jnp.int32),
            pltpu.VMEM((2, 128), jnp.int32),
            pltpu.VMEM((2, 128), jnp.int32),
            pltpu.VMEM((8, 512, HD), F32),
            pltpu.VMEM((8, TENANTS, HD), F32),
            pltpu.VMEM((15, 32, HD), F32),
            pltpu.VMEM((8, 128), F32),
            pltpu.VMEM((16, 8, 128), F32),
            pltpu.VMEM((16, 8, 128), F32),
            pltpu.VMEM((16, 8, 128), F32),
            pltpu.VMEM((128, HD), F32),
            pltpu.VMEM((128, 256), F32),
            pltpu.VMEM((128, HD), F32),
            pltpu.VMEM((128, 128), F32),
            pltpu.VMEM((TENANTS, 512), BF16),
            pltpu.VMEM((128, 128), F32),
            pltpu.VMEM((128, 128), F32),
            dma((12,)), dma, dma((4, ROUNDS)), dma((2, 7)), dma((4,)), dma((4,)), dma, dma,
            dma, dma, dma, dma, dma, dma, pltpu.SemaphoreType.REGULAR((4,)),
        ],
        compiler_params=pltpu.CompilerParams(
            collective_id=0, has_side_effects=True, vmem_limit_bytes=60 * 1024 * 1024
        ),
    )(
        cache_len, tenant_roll, roll_x, queries, cache_k, cache_v, w_key, w_value, ia3_key,
        ia3_value, train_x, upstream, tenant_train.reshape(2, 128), advantage.reshape(2, 128),
    )
    attn_out, gradient, tenant_loss = pl.pallas_call(
        outputs,
        out_shape=(
            jax.ShapeDtypeStruct((16, 1024), BF16),
            jax.ShapeDtypeStruct((2, 128), F32),
            jax.ShapeDtypeStruct((1, TENANTS), F32),
        ),
        in_specs=[vmem, vmem],
        out_specs=(vmem, vmem, vmem),
    )(attn, whole)
    return attn_out, gradient, tenant_loss.reshape(TENANTS)


def solution(mesh):
    finer = Mesh(mesh.devices.reshape(2, 8, 2, 2, 4), AXES)
    placed = (
        P(DP, TENSOR), P(DP, TENSOR), P(DP, None, TENSOR), P(DP, None, TENSOR), P(DP), P(DP),
        P(None, TENSOR), P(None, TENSOR), P(), P(), P(DP_TENSOR, None), P(DP_TENSOR, None),
        P(DP_TENSOR), P(DP_TENSOR),
    )
    return jax.shard_map(
        local_step, mesh=finer, in_specs=placed, out_specs=(P(DP, TENSOR), P(DP, TENSOR), P()),
        check_vma=False,
    )
```

```python
import jax
import jax.numpy as jnp
from jax import lax
from jax.experimental import pallas as pl
from jax.experimental.pallas import tpu as pltpu
from jax.sharding import Mesh
from jax.sharding import PartitionSpec as P

HD = 128
TENANTS = 64
AXES = ("y_hi", "z", "core", "y_lo", "x")
DP = ("y_hi", "z", "core")
TENSOR = ("y_lo", "x")
DP_TENSOR = DP + TENSOR
MESH = pl.DeviceIdType.MESH
F32 = jnp.float32
BF16 = jnp.bfloat16

O, XM, XP, X2, F0, FM, FP, F2 = range(8)
SHIFT = ((0, 0), (0, 3), (0, 1), (0, 2), (1, 0), (1, 3), (1, 1), (1, 2))

HALF = 4096
ZROWS = 1280
ZHALF = ZROWS // 2
QUARTER = ((0, 640), (640, 640), (1280, 768), (2048, 768))


def quarters(block, *which):
    return tuple((block, *QUARTER[k]) for k in which)


LINKS = (
    quarters(XM, 0, 1, 2, 3) + quarters(X2, 0, 2) + ((F2, 3072, 512), (F2, 3584, 512)),
    quarters(XP, 0, 1, 2, 3) + quarters(X2, 1, 3) + ((F2, 1024, 512), (F2, 2560, 512)),
    quarters(F0, 0, 2) + quarters(FM, 0, 1, 2, 3) + ((F2, 0, 512), (F2, 1536, 512)),
    quarters(F0, 1, 3) + quarters(FP, 0, 1, 2, 3) + ((F2, 512, 512), (F2, 2048, 512)),
)
ROUNDS = 8
SENT_AS = (
    {XM: O, X2: XM, F2: FM},
    {XP: O, X2: XP, F2: FP},
    {F0: O, FM: XM, FP: XP, F2: X2},
    {F0: O, FM: XM, FP: XP, F2: X2},
)
Z_SEND = {0: (F0,), 1: (XM, XP), 3: (FM, FP), 4: (X2,)}
Z_TAKE = {2: (F0,), 4: (XM, XP, FM), 5: (FP,), 6: (X2,)}
PRODUCTS = {
    1: (((O, F0), 0, 1280), ((XM, XP), 0, 640), ((O, F0), 1280, 1536), ((XM, XP), 640, 640)),
    2: (((XM, XP), 1280, 768), ((FM, FP), 0, 640), ((O, F0), 2816, 1280)),
    3: (((XM, XP), 2048, 768), ((FM, FP), 640, 640)),
    4: (((X2,), 0, 1280), ((FM, FP), 1280, 768), ((XM, XP), 2816, 1280)),
    5: (((X2,), 1280, 1536), ((FM, FP), 2048, 768), ((FM, FP), 2816, 1280)),
    6: (((F2,), 0, 1536), ((F2,), 3072, 512), ((X2,), 2816, 1280)),
    7: (((F2,), 1536, 1536), ((F2,), 3584, 512)),
}
FINISH = {3: (O, F0), 4: (XM,), 5: (XP,), 6: (FM, FP, X2), 7: (F2,)}
AFTER_Z = ((0, 6), (1, 7))


def dot(a, b):
    return jnp.dot(a, b, preferred_element_type=F32)


def exact_dot(a, b, dims):
    return lax.dot_general(
        a, b, (dims, ((), ())), precision=lax.Precision.HIGHEST, preferred_element_type=F32
    )


def kernel(
    clen, troll, roll_h, q_h, ck_h, cv_h, wk_h, wv_h, ik_h, iv_h, x_h, up_h, tt_h, adv_h,
    attn_o, whole_o,
    wbuf, wv, wk, xh, up, kc, vc, q, rx, ik, iv, tt, adv, tt2, adv2, acc, zmsg, zbuf, fmsg, fbuf, lmine,
    msg, rbuf, smsg, sbuf, qs, sc, mix, snew, mt, lacc, cnt,
    lsem, wsend, wrecv, zrecv, xsend, xrecv, rsend, rrecv, gsend, grecv,
    msend, mrecv, ssend, srecv, known,
):
    y_hi, z, core, y_lo, x = (lax.axis_index(a) for a in AXES)
    t = y_lo * 4 + x
    odd = z % 2
    y = 2 * y_hi + y_lo
    y_up, y_down = (y + 1) % 4, (y + 3) % 4
    sibling = (y_hi, z, 1 - core, y_lo, x)
    z_up = (y_hi, (z + 1) % 8, core, y_lo, x)
    z_down = (y_hi, (z + 7) % 8, core, y_lo, x)
    to_link = (
        (y_hi, z, core, y_lo, (x + 1) % 4),
        (y_hi, z, core, y_lo, (x + 3) % 4),
        (y_up // 2, z, core, y_up % 2, x),
        (y_down // 2, z, core, y_down % 2, x),
    )

    def place(block):
        return (y_lo + SHIFT[block][0]) % 2, (x + SHIFT[block][1]) % 4

    def peer(block):
        py, px = place(block)
        return (y_hi, z, core, py, px)

    def columns(block):
        py, px = place(block)
        return pl.ds(pl.multiple_of((py * 4 + px) * HD, HD), HD)

    def z_peer(step):
        other = (z + step) % 8
        return other, (y_hi, other, core, y_lo, x)

    def remote(src, dst, send, recv, device):
        return pltpu.make_async_remote_copy(
            src_ref=src, dst_ref=dst, send_sem=send, recv_sem=recv,
            device_id=device, device_id_type=MESH,
        )

    own_half = pl.ds(pl.multiple_of(core * HALF, HALF), HALF)
    other_half = pl.ds(pl.multiple_of((1 - core) * HALF, HALF), HALF)
    local = [
        pltpu.make_async_copy(src, dst, lsem.at[k])
        for k, (src, dst) in enumerate(
            (
                (wv_h, wv),
                (x_h.at[:, own_half], xh.at[pl.ds(0, 256)]),
                (tt_h, tt),
                (adv_h, adv),
                (up_h, up.at[pl.ds(0, 256)]),
                (wk_h, wk),
                (roll_h, rx.at[t]),
                (ik_h.at[:, pl.ds(pl.multiple_of(t * HD, HD), HD)], ik),
                (iv_h, iv),
                (q_h, q),
                (ck_h, kc),
                (cv_h, vc),
            )
        )
    ]
    for copy in local:
        copy.start()

    barrier = pltpu.get_barrier_semaphore()
    neighbours = to_link + (z_up, z_down, sibling)

    def tell(semaphore):
        for device in neighbours:
            pl.semaphore_signal(semaphore, inc=1, device_id=device, device_id_type=MESH)

    def hear(semaphore):
        pl.semaphore_wait(semaphore, len(neighbours))

    tell(barrier)
    hear(barrier)

    def rows(first, length):
        return pl.multiple_of((1 - odd) * first + odd * (HALF - first - length), 128)

    def link_copy(link, r):
        block, first, length = LINKS[link][r]
        source = SENT_AS[link][block]
        row = rows(first, length)
        if source == O:
            src = wv_h.at[pl.ds(pl.multiple_of(core * HALF + row, 128), length)]
        else:
            src = wbuf.at[source - 1, pl.ds(row, length)]
        return remote(
            src, wbuf.at[block - 1, pl.ds(row, length)], wsend, wrecv.at[link, r], to_link[link]
        )

    def z_copy(block, h, base):
        ref = wbuf.at[block - 1, pl.ds(pl.multiple_of(base + h * ZHALF, 128), ZHALF)]
        return remote(ref, ref, wsend, zrecv.at[h, block - 1], z_up if h == 0 else z_down)

    z_sent = odd * (HALF - ZROWS)
    z_taken = (1 - odd) * (HALF - ZROWS)

    def issue(r):
        for link in range(4):
            if (link, r) not in AFTER_Z:
                link_copy(link, r).start()

    issue(0)
    issue(1)
    tell(known.at[0])
    exchange = [
        remote(src, dst, xsend.at[k], xrecv.at[k], sibling)
        for k, (src, dst) in enumerate(
            (
                (x_h.at[:, other_half], xh.at[pl.ds(256, 256)]),
                (up_h, up.at[pl.ds(256, 256)]),
                (tt_h, tt2),
                (adv_h, adv2),
            )
        )
    ]
    for copy in exchange:
        copy.start()
    beside_y = (y_hi, z, core, 1 - y_lo, x)
    RELAY = (
        ((0, O, 0, 1024), (1, O, 0, 1024), (4, O, 0, 1024)),
        ((0, XM, 0, 512), (1, XP, 512, 512), (0, F0, 0, 1024), (1, F0, 0, 1024)),
        ((4, X2, 0, 1024),),
    )

    def relay(step):
        copies = []
        for k, (to, block, first, width) in enumerate(RELAY[step]):
            py, px = place(block)
            here = py * 4 + px
            slot = rx.at[here, :, pl.ds(first, width)]
            source = roll_h if block == O else slot
            device = beside_y if to == 4 else to_link[to]
            copies.append(remote(source, slot, rsend, rrecv.at[3 * step + step // 2 + k], device))
        return copies

    for copy in relay(0):
        copy.start()

    def part_of(block, row, length):
        if block == O:
            return wv[pl.ds(pl.multiple_of(core * HALF + row, 128), length), :]
        return wbuf[block - 1, pl.ds(row, length), :]

    def product(blocks, first, length, new):
        row = rows(first, length)
        parts = [part_of(block, row, length) for block in blocks]
        both = parts[0] if len(parts) == 1 else jnp.concatenate(parts, axis=1)
        result = dot(xh[:, pl.ds(row, length)], both)
        for k, block in enumerate(blocks):
            if new:
                acc[block] = result[:, k * HD : (k + 1) * HD]
            else:
                acc[block] += result[:, k * HD : (k + 1) * HD]

    def z_copies(block):
        copies = []
        for step in range(1, 8):
            other, device = z_peer(step)
            if block == F2:
                pair = fmsg.at[other], fbuf.at[z]
            else:
                pair = zmsg.at[block, other], zbuf.at[block, z]
            copies.append(remote(*pair, gsend, grecv.at[block], device))
        return copies

    def fold(block):
        weighted = acc[block] * up[:, columns(block)].astype(F32)
        high = weighted.astype(BF16)
        low = (weighted - high.astype(F32)).astype(BF16)
        return dot(mt[...], high) + dot(mt[...], low)

    def finish(block, first=False):
        sums = fold(block)
        part = sums * iv[:, columns(block)]
        for k in range(8):
            if block == F2:
                fmsg[k, 0:4, :] = sums[4 * k : 4 * k + 4, :]
                fmsg[k, 4:8, :] = sums[32 + 4 * k : 36 + 4 * k, :]
            else:
                zmsg[block, k, 0:4, :] = sums[4 * k : 4 * k + 4, :]
                zmsg[block, k, 4:8, :] = sums[32 + 4 * k : 36 + 4 * k, :]
        if block == F2:
            lacc[0:64, :] = part
            mine = lmine[...] + jnp.where(
                tile_row == 4, exact_dot(ones, lacc[...], ((1,), (1,))), 0.0
            )
            for k in range(8):
                fmsg[k, 8:16, :] = mine
        elif first:
            lacc[0:64, :] = part
        else:
            lacc[0:64, :] += part
        for copy in z_copies(block):
            copy.start()
        if block == F2:
            fbuf[z] = fmsg[z]
        else:
            zbuf[block, z] = zmsg[block, z]

    def over_z(block):
        buf = fbuf if block == F2 else zbuf.at[block]
        some = buf.at[pl.ds(0, 7)]
        remote(some, some, gsend, grecv.at[block], sibling).wait_recv()
        total = buf[0]
        for k in range(1, 8):
            total = total + buf[k]
        for k in range(2):
            msg[block, k, 0:4, :] = total[4 * k : 4 * k + 4, :]
        return total

    def table():
        for k in (2, 3):
            local[k].wait()
        for k in (2, 3):
            exchange[k].wait_recv()
        tenant = lax.broadcasted_iota(jnp.int32, (64, 128), 0)
        hits = []
        for k in range(4):
            labels, gains = (tt, adv) if k < 2 else (tt2, adv2)
            k2 = k % 2
            hits.append(
                (tenant == jnp.broadcast_to(labels[k2 : k2 + 1, :], (64, 128))).astype(F32)
            )
            gain = jnp.broadcast_to(gains[k2 : k2 + 1, :].astype(F32), (64, 128))
            mt[:, k * 128 : (k + 1) * 128] = (hits[k] * gain).astype(BF16)
        cnt[0:64, :] = hits[0] + hits[1]
        cnt[64:128, :] = jnp.zeros((64, 128), F32)
        lacc[64:128, :] = jnp.zeros((64, 128), F32)

    scale = 1.0 / jnp.sqrt(F32(HD))

    def spread(h, transposed=False):
        shape = (16, 128) if transposed else (128, 16)
        pair = lax.broadcasted_iota(jnp.int32, shape, 1 if transposed else 0)
        row = lax.broadcasted_iota(jnp.int32, shape, 0 if transposed else 1)
        if h is None:
            return (pair // 8 == row).astype(F32).astype(BF16)
        return (pair == row * 8 + h).astype(F32).astype(BF16)

    def project():
        for k in (5, 6, 7, 9):
            local[k].wait()
        relay(2)[0].wait_recv()
        key_sum = jnp.zeros((16, HD), F32)
        value_sum = jnp.zeros((16, HD), F32)
        for k in range(8):
            part = rx[k]
            key_sum = key_sum + dot(part, wk[k * 1024 : (k + 1) * 1024, :])
            value_sum = value_sum + dot(part, wv[k * 1024 : (k + 1) * 1024, :])
        row = lax.broadcasted_iota(jnp.int32, (16, TENANTS), 0)
        owner = jnp.zeros((16, TENANTS), jnp.int32)
        for r in range(16):
            owner = jnp.where(row == r, troll[r], owner)
        onehot = (owner == lax.broadcasted_iota(jnp.int32, (16, TENANTS), 1)).astype(F32)
        key_gain = exact_dot(onehot, ik[...], ((1,), (0,)))
        value_gain = exact_dot(onehot, iv[:, columns(O)], ((1,), (0,)))
        key_new = (key_sum * key_gain).astype(BF16)
        value_new = (value_sum * value_gain).astype(BF16)
        queries = jnp.zeros((128, HD), F32)
        for h in range(8):
            queries = queries + dot(spread(h), q[:, h * HD : (h + 1) * HD])
        qs[...] = queries
        each = spread(None)
        snew[...] = jnp.broadcast_to(
            jnp.sum(queries * dot(each, key_new), axis=1, keepdims=True) * scale, (128, 128)
        )
        mix[...] = dot(each, value_new)

    def score():
        local[10].wait()
        place_in_cache = lax.broadcasted_iota(jnp.int32, (8, 256), 1)
        for r in range(16):
            s = lax.dot_general(
                qs[r * 8 : (r + 1) * 8, :].astype(BF16), kc[r], (((1,), (1,)), ((), ())),
                preferred_element_type=F32,
            ) * scale
            sc[r * 8 : (r + 1) * 8, :] = jnp.where(place_in_cache < clen[r], s, -jnp.inf)

    def normalise():
        s = sc[...]
        new = snew[:, 0:1]
        highest = jnp.maximum(jnp.max(s, axis=1, keepdims=True), new)
        expo = jnp.exp(s - highest)
        expo_new = jnp.exp(new - highest)
        denominator = jnp.sum(expo, axis=1, keepdims=True) + expo_new
        sc[...] = (expo / denominator).astype(BF16).astype(F32)
        mix[...] = (expo_new / denominator).astype(BF16).astype(F32) * mix[...]

    def mixture():
        local[11].wait()
        for r in range(16):
            rows = slice(r * 8, (r + 1) * 8)
            mix[rows, :] += dot(sc[rows, :].astype(BF16), vc[r])
        mixed = mix[...].astype(BF16)
        for h in range(8):
            attn_o[:, h * HD : (h + 1) * HD] = dot(spread(h, True), mixed).astype(BF16)

    ones = jnp.ones((8, 128), F32)
    tile_row = lax.broadcasted_iota(jnp.int32, (8, 128), 0)

    def loss_and_count():
        loss_row = exact_dot(ones, lacc[...], ((1,), (1,)))
        count_row = exact_dot(ones, cnt[...], ((1,), (1,)))
        return jnp.where(tile_row == 4, loss_row, jnp.where(tile_row == 5, count_row, 0.0))

    beside = {2: project, 3: score, 4: normalise, 5: mixture}

    hear(known.at[0])
    tell(known.at[1])
    seen = set()
    for r in range(ROUNDS):
        for link in range(4):
            link_copy(link, r).wait_recv()
        if r + 2 < ROUNDS:
            issue(r + 2)
        for block in Z_SEND.get(r, ()):
            for h in range(2):
                z_copy(block, h, z_sent).start()
        if r < 3:
            hear(known.at[r + 1])
            if r < 2:
                tell(known.at[r + 2])
        if r < 2:
            for copy in relay(r):
                copy.wait_recv()
            for copy in relay(r + 1):
                copy.start()
        if r == 0:
            table()
            for k in (0, 1, 4, 8):
                local[k].wait()
        if r == 1:
            exchange[0].wait_recv()
            exchange[1].wait_recv()
        for block in Z_TAKE.get(r, ()):
            for h in range(2):
                z_copy(block, h, z_taken).wait_recv()
        for link, later in AFTER_Z:
            if later == r + 2:
                link_copy(link, later).start()
        for blocks, first, length in PRODUCTS.get(r, ()):
            product(blocks, first, length, blocks[0] not in seen)
            seen.update(blocks)
        if r in beside:
            beside[r]()
        for block in FINISH.get(r, ()):
            finish(block, block == O)
        if r == ROUNDS - 2:
            lmine[...] = loss_and_count()
        if r == ROUNDS - 1:
            for block in range(F2):
                over_z(block)

    last = over_z(F2)
    for block in range(8):
        for k in range(2):
            msg[block, k, 4:8, :] = last[12:16, :]
    group = y * 4 + x
    for block in range(8):
        py, px = place(block)
        for k, high in enumerate((y_hi, 1 - y_hi)):
            if block + k > 0:
                remote(
                    msg.at[block, high], rbuf.at[group], msend, mrecv, (high, z, core, py, px)
                ).start()
    rbuf[group] = msg[O, y_hi]
    some = rbuf.at[pl.ds(0, 15)]
    remote(some, some, msend, mrecv, sibling).wait_recv()
    plane = rbuf[0]
    for k in range(1, 16):
        plane = plane + rbuf[k]
    smsg[...] = plane
    across = remote(smsg, sbuf, ssend, srecv, sibling)
    across.start()
    across.wait_recv()
    whole = plane + sbuf[...]
    whole_o[...] = whole

    for copy in exchange:
        copy.wait_send()
    remote(rx.at[pl.ds(0, 7)], rx.at[pl.ds(0, 7)], rsend, srecv, sibling).wait_send()
    remote(wbuf, wbuf, wsend, srecv, sibling).wait_send()
    across.wait_send()
    remote(zbuf.at[pl.ds(0, 7), pl.ds(0, 7)], zbuf.at[pl.ds(0, 7), pl.ds(0, 7)], gsend, srecv, sibling).wait_send()
    remote(fbuf.at[pl.ds(0, 7)], fbuf.at[pl.ds(0, 7)], gsend, srecv, sibling).wait_send()
    remote(rbuf.at[pl.ds(0, 15)], rbuf.at[pl.ds(0, 15)], msend, mrecv, sibling).wait_send()


def outputs(attn, whole, attn_o, grad_o, loss_o):
    core = lax.axis_index("core")
    d = lax.axis_index("y_hi") * 16 + lax.axis_index("z") * 2 + core
    attn_o[...] = attn[...]
    divisor = jnp.maximum(whole[5:6, :], 1.0)
    loss_o[...] = (-whole[4:5, :] / divisor)[:, 0:TENANTS]
    lane = lax.broadcasted_iota(jnp.int32, (2, 128), 1)
    row = lax.broadcasted_iota(jnp.int32, (2, 128), 0)
    own = jnp.sum(
        jnp.where(lane == 2 * d + row, jnp.broadcast_to(divisor, (2, 128)), 0.0),
        axis=1, keepdims=True,
    )
    grad_o[...] = -jnp.where(core == 0, whole[0:2, :], whole[2:4, :]) / own


def local_step(
    roll_x, queries, cache_k, cache_v, cache_len, tenant_roll, w_key, w_value, ia3_key,
    ia3_value, train_x, upstream, tenant_train, advantage,
):
    smem = pl.BlockSpec(memory_space=pltpu.SMEM)
    vmem = pl.BlockSpec(memory_space=pltpu.VMEM)
    anywhere = pl.BlockSpec(memory_space=pl.ANY)
    dma = pltpu.SemaphoreType.DMA
    attn, whole = pl.pallas_call(
        kernel,
        out_shape=(
            jax.ShapeDtypeStruct((16, 1024), BF16),
            jax.ShapeDtypeStruct((8, 128), F32),
        ),
        in_specs=[smem, smem] + [anywhere] * 12,
        out_specs=(vmem, vmem),
        scratch_shapes=[
            pltpu.VMEM((7, HALF, HD), BF16),
            pltpu.VMEM((2 * HALF, HD), BF16),
            pltpu.VMEM((2 * HALF, HD), BF16),
            pltpu.VMEM((512, HALF), BF16),
            pltpu.VMEM((512, 1024), BF16),
            pltpu.VMEM((16, 256, HD), BF16),
            pltpu.VMEM((16, 256, HD), BF16),
            pltpu.VMEM((16, 1024), BF16),
            pltpu.VMEM((8, 16, 1024), BF16),
            pltpu.VMEM((TENANTS, HD), F32),
            pltpu.VMEM((TENANTS, 1024), F32),
            pltpu.VMEM((2, 128), jnp.int32),
            pltpu.VMEM((2, 128), jnp.int32),
            pltpu.VMEM((2, 128), jnp.int32),
            pltpu.VMEM((2, 128), jnp.int32),
            pltpu.VMEM((8, 512, HD), F32),
            pltpu.VMEM((7, 8, 8, HD), F32),
            pltpu.VMEM((7, 8, 8, HD), F32),
            pltpu.VMEM((8, 16, HD), F32),
            pltpu.VMEM((8, 16, HD), F32),
            pltpu.VMEM((8, 128), F32),
            pltpu.VMEM((8, 2, 8, HD), F32),
            pltpu.VMEM((16, 8, HD), F32),
            pltpu.VMEM((8, HD), F32),
            pltpu.VMEM((8, HD), F32),
            pltpu.VMEM((128, HD), F32),
            pltpu.VMEM((128, 256), F32),
            pltpu.VMEM((128, HD), F32),
            pltpu.VMEM((128, 128), F32),
            pltpu.VMEM((TENANTS, 512), BF16),
            pltpu.VMEM((128, 128), F32),
            pltpu.VMEM((128, 128), F32),
            dma((12,)), dma, dma((4, ROUNDS)), dma((2, 7)), dma((4,)), dma((4,)), dma, dma((8,)),
            dma, dma((8,)), dma, dma, dma, dma, pltpu.SemaphoreType.REGULAR((4,)),
        ],
        compiler_params=pltpu.CompilerParams(
            collective_id=0, has_side_effects=True, vmem_limit_bytes=60 * 1024 * 1024
        ),
    )(
        cache_len, tenant_roll, roll_x, queries, cache_k, cache_v, w_key, w_value, ia3_key,
        ia3_value, train_x, upstream, tenant_train.reshape(2, 128), advantage.reshape(2, 128),
    )
    attn_out, gradient, tenant_loss = pl.pallas_call(
        outputs,
        out_shape=(
            jax.ShapeDtypeStruct((16, 1024), BF16),
            jax.ShapeDtypeStruct((2, 128), F32),
            jax.ShapeDtypeStruct((1, TENANTS), F32),
        ),
        in_specs=[vmem, vmem],
        out_specs=(vmem, vmem, vmem),
    )(attn, whole)
    return attn_out, gradient, tenant_loss.reshape(TENANTS)


def solution(mesh):
    finer = Mesh(mesh.devices.reshape(2, 8, 2, 2, 4), AXES)
    placed = (
        P(DP, TENSOR), P(DP, TENSOR), P(DP, None, TENSOR), P(DP, None, TENSOR), P(DP), P(DP),
        P(None, TENSOR), P(None, TENSOR), P(), P(), P(DP_TENSOR, None), P(DP_TENSOR, None),
        P(DP_TENSOR), P(DP_TENSOR),
    )
    return jax.shard_map(
        local_step, mesh=finer, in_specs=placed, out_specs=(P(DP, TENSOR), P(DP, TENSOR), P()),
        check_vma=False,
    )
```

```python
import jax
import jax.numpy as jnp
from jax import lax
from jax.experimental import pallas as pl
from jax.experimental.pallas import tpu as pltpu
from jax.sharding import Mesh
from jax.sharding import PartitionSpec as P

HD = 128
TENANTS = 64
AXES = ("y_hi", "z", "core", "y_lo", "x")
DP = ("y_hi", "z", "core")
TENSOR = ("y_lo", "x")
DP_TENSOR = DP + TENSOR
MESH = pl.DeviceIdType.MESH
F32 = jnp.float32
BF16 = jnp.bfloat16

O, XM, XP, X2, F0, FM, FP, F2 = range(8)
SHIFT = ((0, 0), (0, 3), (0, 1), (0, 2), (1, 0), (1, 3), (1, 1), (1, 2))
INVERSE = (O, XP, XM, X2, F0, FP, FM, F2)

HALF = 4096
ZROWS = 1280
ZHALF = ZROWS // 2
QUARTER = ((0, 640), (640, 640), (1280, 768), (2048, 768))


def quarters(block, *which):
    return tuple((block, *QUARTER[k]) for k in which)


LINKS = (
    quarters(XM, 0, 1, 2, 3) + quarters(X2, 0, 2) + ((F2, 3072, 512), (F2, 3584, 512)),
    quarters(XP, 0, 1, 2, 3) + quarters(X2, 1, 3) + ((F2, 1024, 512), (F2, 2560, 512)),
    quarters(F0, 0, 2) + quarters(FM, 0, 1, 2, 3) + ((F2, 0, 512), (F2, 1536, 512)),
    quarters(F0, 1, 3) + quarters(FP, 0, 1, 2, 3) + ((F2, 512, 512), (F2, 2048, 512)),
)
ROUNDS = 8
SENT_AS = (
    {XM: O, X2: XM, F2: FM},
    {XP: O, X2: XP, F2: FP},
    {F0: O, FM: XM, FP: XP, F2: X2},
    {F0: O, FM: XM, FP: XP, F2: X2},
)
Z_SEND = {0: (F0,), 1: (XM, XP), 3: (FM, FP), 4: (X2,)}
Z_TAKE = {2: (F0,), 4: (XM, XP, FM), 5: (FP,), 6: (X2,)}
PRODUCTS = {
    1: (((O, F0), 0, 1280), ((XM, XP), 0, 640), ((O, F0), 1280, 1536), ((XM, XP), 640, 640)),
    2: (((XM, XP), 1280, 768), ((FM, FP), 0, 640), ((O, F0), 2816, 1280)),
    3: (((XM, XP), 2048, 768), ((FM, FP), 640, 640)),
    4: (((X2,), 0, 1280), ((FM, FP), 1280, 768), ((XM, XP), 2816, 1280)),
    5: (((X2,), 1280, 1536), ((FM, FP), 2048, 768), ((FM, FP), 2816, 1280)),
    6: (((F2,), 0, 1536), ((F2,), 3072, 512), ((X2,), 2816, 1280)),
    7: (((F2,), 1536, 1536), ((F2,), 3584, 512)),
}
FINISH = {3: (O, F0), 4: (XM,), 5: (XP,), 6: (FM, FP, X2), 7: (F2,)}
AFTER_Z = ((0, 6), (1, 7))


def dot(a, b):
    return jnp.dot(a, b, preferred_element_type=F32)


def exact_dot(a, b, dims):
    return lax.dot_general(
        a, b, (dims, ((), ())), precision=lax.Precision.HIGHEST, preferred_element_type=F32
    )


def kernel(
    clen, troll, roll_h, q_h, ck_h, cv_h, wk_h, wv_h, ik_h, iv_h, x_h, up_h, tt_h, adv_h,
    attn_o, whole_o,
    wbuf, wv, wk, xh, up, kc, vc, q, rx, ik, iv, tt, adv, tt2, adv2, acc, sbuf, gbuf, lmine, lbuf,
    msg, rbuf, qs, sc, mix, snew, mt, lacc, cnt,
    lsem, wsend, wrecv, zrecv, xsend, xrecv, rsend, rrecv, gsend, grecv,
    lsend, lrecv, msend, mrecv, known,
):
    y_hi, z, core, y_lo, x = (lax.axis_index(a) for a in AXES)
    t = y_lo * 4 + x
    odd = z % 2
    y = 2 * y_hi + y_lo
    y_up, y_down = (y + 1) % 4, (y + 3) % 4
    sibling = (y_hi, z, 1 - core, y_lo, x)
    z_up = (y_hi, (z + 1) % 8, core, y_lo, x)
    z_down = (y_hi, (z + 7) % 8, core, y_lo, x)
    to_link = (
        (y_hi, z, core, y_lo, (x + 1) % 4),
        (y_hi, z, core, y_lo, (x + 3) % 4),
        (y_up // 2, z, core, y_up % 2, x),
        (y_down // 2, z, core, y_down % 2, x),
    )

    def place(block):
        return (y_lo + SHIFT[block][0]) % 2, (x + SHIFT[block][1]) % 4

    def peer(block):
        py, px = place(block)
        return (y_hi, z, core, py, px)

    def columns(block):
        py, px = place(block)
        return pl.ds(pl.multiple_of((py * 4 + px) * HD, HD), HD)

    def plane_peer(step):
        other = (y * 4 + x + step) % 16
        return other, (other // 8, z, core, (other // 4) % 2, other % 4)

    def column_peer(step):
        other = (z * 2 + core + step) % 16
        return other, (y_hi, other // 2, other % 2, y_lo, x)

    def remote(src, dst, send, recv, device):
        return pltpu.make_async_remote_copy(
            src_ref=src, dst_ref=dst, send_sem=send, recv_sem=recv,
            device_id=device, device_id_type=MESH,
        )

    own_half = pl.ds(pl.multiple_of(core * HALF, HALF), HALF)
    other_half = pl.ds(pl.multiple_of((1 - core) * HALF, HALF), HALF)
    local = [
        pltpu.make_async_copy(src, dst, lsem.at[k])
        for k, (src, dst) in enumerate(
            (
                (wv_h, wv),
                (x_h.at[:, own_half], xh.at[pl.ds(0, 256)]),
                (tt_h, tt),
                (adv_h, adv),
                (up_h, up.at[pl.ds(0, 256)]),
                (wk_h, wk),
                (roll_h, rx.at[t]),
                (ik_h.at[:, pl.ds(pl.multiple_of(t * HD, HD), HD)], ik),
                (iv_h, iv),
                (q_h, q),
                (ck_h, kc),
                (cv_h, vc),
            )
        )
    ]
    barrier = pltpu.get_barrier_semaphore()
    neighbours = to_link + (z_up, z_down, sibling)

    def tell(semaphore):
        for device in neighbours:
            pl.semaphore_signal(semaphore, inc=1, device_id=device, device_id_type=MESH)

    def hear(semaphore):
        pl.semaphore_wait(semaphore, len(neighbours))

    tell(barrier)
    for copy in local:
        copy.start()
    hear(barrier)

    def rows(first, length):
        return pl.multiple_of((1 - odd) * first + odd * (HALF - first - length), 128)

    def link_copy(link, r):
        block, first, length = LINKS[link][r]
        source = SENT_AS[link][block]
        row = rows(first, length)
        if source == O:
            src = wv_h.at[pl.ds(pl.multiple_of(core * HALF + row, 128), length)]
        else:
            src = wbuf.at[source - 1, pl.ds(row, length)]
        return remote(
            src, wbuf.at[block - 1, pl.ds(row, length)], wsend, wrecv.at[link, r], to_link[link]
        )

    def z_copy(block, h, base):
        ref = wbuf.at[block - 1, pl.ds(pl.multiple_of(base + h * ZHALF, 128), ZHALF)]
        return remote(ref, ref, wsend, zrecv.at[h, block - 1], z_up if h == 0 else z_down)

    z_sent = odd * (HALF - ZROWS)
    z_taken = (1 - odd) * (HALF - ZROWS)

    def issue(r):
        for link in range(4):
            if (link, r) not in AFTER_Z:
                link_copy(link, r).start()

    issue(0)
    issue(1)
    tell(known.at[0])
    exchange = [
        remote(src, dst, xsend.at[k], xrecv.at[k], sibling)
        for k, (src, dst) in enumerate(
            (
                (x_h.at[:, other_half], xh.at[pl.ds(256, 256)]),
                (up_h, up.at[pl.ds(256, 256)]),
                (tt_h, tt2),
                (adv_h, adv2),
            )
        )
    ]
    for copy in exchange:
        copy.start()
    beside_y = (y_hi, z, core, 1 - y_lo, x)
    RELAY = (
        ((0, O, 0, 1024), (1, O, 0, 1024), (4, O, 0, 1024)),
        ((0, XM, 0, 512), (1, XP, 512, 512), (0, F0, 0, 1024), (1, F0, 0, 1024)),
        ((4, X2, 0, 1024),),
    )

    def relay(step):
        copies = []
        for k, (to, block, first, width) in enumerate(RELAY[step]):
            py, px = place(block)
            here = py * 4 + px
            slot = rx.at[here, :, pl.ds(first, width)]
            source = roll_h if block == O else slot
            device = beside_y if to == 4 else to_link[to]
            copies.append(remote(source, slot, rsend, rrecv.at[3 * step + step // 2 + k], device))
        return copies

    for copy in relay(0):
        copy.start()

    def part_of(block, row, length):
        if block == O:
            return wv[pl.ds(pl.multiple_of(core * HALF + row, 128), length), :]
        return wbuf[block - 1, pl.ds(row, length), :]

    def product(blocks, first, length, new):
        row = rows(first, length)
        parts = [part_of(block, row, length) for block in blocks]
        both = parts[0] if len(parts) == 1 else jnp.concatenate(parts, axis=1)
        result = dot(xh[:, pl.ds(row, length)], both)
        for k, block in enumerate(blocks):
            if new:
                acc[block] = result[:, k * HD : (k + 1) * HD]
            else:
                acc[block] += result[:, k * HD : (k + 1) * HD]

    def sum_copies(block):
        copies = []
        for k, high in enumerate((y_hi, 1 - y_hi)):
            slot = INVERSE[block] + 8 * k
            if slot > 0:
                py, px = place(block)
                copies.append(
                    remote(
                        sbuf.at[block, pl.ds(pl.multiple_of(32 * high, 32), 32)],
                        gbuf.at[slot - 1], gsend, grecv, (high, z, core, py, px),
                    )
                )
        return copies

    def finish(block, first=False):
        weighted = acc[block] * up[:, columns(block)].astype(F32)
        high = weighted.astype(BF16)
        low = (weighted - high.astype(F32)).astype(BF16)
        sums = dot(mt[...], high) + dot(mt[...], low)
        sbuf[block] = sums
        for copy in sum_copies(block):
            copy.start()
        part = sums * iv[:, columns(block)]
        if first:
            lacc[0:64, :] = part
        else:
            lacc[0:64, :] += part

    def table():
        for k in (2, 3):
            local[k].wait()
        for k in (2, 3):
            exchange[k].wait_recv()
        tenant = lax.broadcasted_iota(jnp.int32, (64, 128), 0)
        hits = []
        for k in range(4):
            labels, gains = (tt, adv) if k < 2 else (tt2, adv2)
            k2 = k % 2
            hits.append(
                (tenant == jnp.broadcast_to(labels[k2 : k2 + 1, :], (64, 128))).astype(F32)
            )
            gain = jnp.broadcast_to(gains[k2 : k2 + 1, :].astype(F32), (64, 128))
            mt[:, k * 128 : (k + 1) * 128] = (hits[k] * gain).astype(BF16)
        cnt[0:64, :] = hits[0] + hits[1]
        cnt[64:128, :] = jnp.zeros((64, 128), F32)
        lacc[64:128, :] = jnp.zeros((64, 128), F32)

    scale = 1.0 / jnp.sqrt(F32(HD))

    def spread(h, transposed=False):
        shape = (16, 128) if transposed else (128, 16)
        pair = lax.broadcasted_iota(jnp.int32, shape, 1 if transposed else 0)
        row = lax.broadcasted_iota(jnp.int32, shape, 0 if transposed else 1)
        if h is None:
            return (pair // 8 == row).astype(F32).astype(BF16)
        return (pair == row * 8 + h).astype(F32).astype(BF16)

    def project():
        for k in (5, 6, 7, 9):
            local[k].wait()
        relay(2)[0].wait_recv()
        key_sum = jnp.zeros((16, HD), F32)
        value_sum = jnp.zeros((16, HD), F32)
        for k in range(8):
            part = rx[k]
            key_sum = key_sum + dot(part, wk[k * 1024 : (k + 1) * 1024, :])
            value_sum = value_sum + dot(part, wv[k * 1024 : (k + 1) * 1024, :])
        row = lax.broadcasted_iota(jnp.int32, (16, TENANTS), 0)
        owner = jnp.zeros((16, TENANTS), jnp.int32)
        for r in range(16):
            owner = jnp.where(row == r, troll[r], owner)
        onehot = (owner == lax.broadcasted_iota(jnp.int32, (16, TENANTS), 1)).astype(F32)
        key_gain = exact_dot(onehot, ik[...], ((1,), (0,)))
        value_gain = exact_dot(onehot, iv[:, columns(O)], ((1,), (0,)))
        key_new = (key_sum * key_gain).astype(BF16)
        value_new = (value_sum * value_gain).astype(BF16)
        queries = jnp.zeros((128, HD), F32)
        for h in range(8):
            queries = queries + dot(spread(h), q[:, h * HD : (h + 1) * HD])
        qs[...] = queries
        each = spread(None)
        snew[...] = jnp.broadcast_to(
            jnp.sum(queries * dot(each, key_new), axis=1, keepdims=True) * scale, (128, 128)
        )
        mix[...] = dot(each, value_new)

    def score():
        local[10].wait()
        place_in_cache = lax.broadcasted_iota(jnp.int32, (8, 256), 1)
        for r in range(16):
            s = lax.dot_general(
                qs[r * 8 : (r + 1) * 8, :].astype(BF16), kc[r], (((1,), (1,)), ((), ())),
                preferred_element_type=F32,
            ) * scale
            sc[r * 8 : (r + 1) * 8, :] = jnp.where(place_in_cache < clen[r], s, -jnp.inf)

    def normalise():
        s = sc[...]
        new = snew[:, 0:1]
        highest = jnp.maximum(jnp.max(s, axis=1, keepdims=True), new)
        expo = jnp.exp(s - highest)
        expo_new = jnp.exp(new - highest)
        denominator = jnp.sum(expo, axis=1, keepdims=True) + expo_new
        sc[...] = (expo / denominator).astype(BF16).astype(F32)
        mix[...] = (expo_new / denominator).astype(BF16).astype(F32) * mix[...]

    def mixture():
        local[11].wait()
        for r in range(16):
            rows = slice(r * 8, (r + 1) * 8)
            mix[rows, :] += dot(sc[rows, :].astype(BF16), vc[r])
        mixed = mix[...].astype(BF16)
        for h in range(8):
            attn_o[:, h * HD : (h + 1) * HD] = dot(spread(h, True), mixed).astype(BF16)

    ones = jnp.ones((8, 128), F32)
    tile_row = lax.broadcasted_iota(jnp.int32, (8, 128), 0)

    def loss_and_count():
        loss_row = exact_dot(ones, lacc[...], ((1,), (1,)))
        count_row = exact_dot(ones, cnt[...], ((1,), (1,)))
        return jnp.where(tile_row == 2, loss_row, jnp.where(tile_row == 3, count_row, 0.0))

    beside = {2: project, 3: score, 4: normalise, 5: mixture}

    hear(known.at[0])
    tell(known.at[1])
    seen = set()
    for r in range(ROUNDS):
        for link in range(4):
            link_copy(link, r).wait_recv()
        if r + 2 < ROUNDS:
            issue(r + 2)
        for block in Z_SEND.get(r, ()):
            for h in range(2):
                z_copy(block, h, z_sent).start()
        if r < 3:
            hear(known.at[r + 1])
            if r < 2:
                tell(known.at[r + 2])
        if r < 2:
            for copy in relay(r):
                copy.wait_recv()
            for copy in relay(r + 1):
                copy.start()
        if r == 0:
            table()
            for k in (0, 1, 4, 8):
                local[k].wait()
        if r == 1:
            exchange[0].wait_recv()
            exchange[1].wait_recv()
        for block in Z_TAKE.get(r, ()):
            for h in range(2):
                z_copy(block, h, z_taken).wait_recv()
        for link, later in AFTER_Z:
            if later == r + 2:
                link_copy(link, later).start()
        for blocks, first, length in PRODUCTS.get(r, ()):
            product(blocks, first, length, blocks[0] not in seen)
            seen.update(blocks)
        if r in beside:
            beside[r]()
        for block in FINISH.get(r, ()):
            finish(block, block in (O, F2))
        if r == ROUNDS - 2:
            lmine[...] = loss_and_count()

    group = y * 4 + x
    mine = lmine[...] + jnp.where(tile_row == 2, exact_dot(ones, lacc[...], ((1,), (1,))), 0.0)
    lmine[...] = mine
    for step in range(1, 16):
        remote(lmine, lbuf.at[group], lsend, lrecv, plane_peer(step)[1]).start()
    lbuf[group] = mine

    remote(gbuf, gbuf, gsend, grecv, sibling).wait_recv()
    total = sbuf[O, pl.ds(pl.multiple_of(32 * y_hi, 32), 32), :]
    for k in range(15):
        total = total + gbuf[k]
    remote(lbuf.at[pl.ds(0, 15)], lbuf.at[pl.ds(0, 15)], lsend, lrecv, sibling).wait_recv()
    plane = lbuf[0]
    for k in range(1, 16):
        plane = plane + lbuf[k]
    for k in range(16):
        msg[k] = plane
        msg[k, 0:2, :] = total[2 * k : 2 * k + 2, :]
    own = z * 2 + core
    for step in range(1, 16):
        other, device = column_peer(step)
        remote(msg.at[other], rbuf.at[own], msend, mrecv, device).start()
    rbuf[own] = msg[own]
    remote(rbuf.at[pl.ds(0, 15)], rbuf.at[pl.ds(0, 15)], msend, mrecv, sibling).wait_recv()
    whole = rbuf[0]
    for k in range(1, 16):
        whole = whole + rbuf[k]
    whole_o[...] = whole

    for copy in exchange:
        copy.wait_send()
    remote(rx.at[pl.ds(0, 7)], rx.at[pl.ds(0, 7)], rsend, grecv, sibling).wait_send()
    remote(wbuf, wbuf, wsend, grecv, sibling).wait_send()
    remote(gbuf, gbuf, gsend, grecv, sibling).wait_send()
    remote(lbuf.at[pl.ds(0, 15)], lbuf.at[pl.ds(0, 15)], lsend, lrecv, sibling).wait_send()
    remote(rbuf.at[pl.ds(0, 15)], rbuf.at[pl.ds(0, 15)], msend, mrecv, sibling).wait_send()


def outputs(attn, whole, attn_o, grad_o, loss_o):
    d = lax.axis_index("y_hi") * 16 + lax.axis_index("z") * 2 + lax.axis_index("core")
    attn_o[...] = attn[...]
    divisor = jnp.maximum(whole[3:4, :], 1.0)
    loss_o[...] = (-whole[2:3, :] / divisor)[:, 0:TENANTS]
    lane = lax.broadcasted_iota(jnp.int32, (2, 128), 1)
    row = lax.broadcasted_iota(jnp.int32, (2, 128), 0)
    own = jnp.sum(
        jnp.where(lane == 2 * d + row, jnp.broadcast_to(divisor, (2, 128)), 0.0),
        axis=1, keepdims=True,
    )
    grad_o[...] = -whole[0:2, :] / own


def local_step(
    roll_x, queries, cache_k, cache_v, cache_len, tenant_roll, w_key, w_value, ia3_key,
    ia3_value, train_x, upstream, tenant_train, advantage,
):
    smem = pl.BlockSpec(memory_space=pltpu.SMEM)
    vmem = pl.BlockSpec(memory_space=pltpu.VMEM)
    anywhere = pl.BlockSpec(memory_space=pl.ANY)
    dma = pltpu.SemaphoreType.DMA
    attn, whole = pl.pallas_call(
        kernel,
        out_shape=(
            pltpu.VMEM((16, 1024), BF16),
            pltpu.VMEM((8, 128), F32),
        ),
        in_specs=[smem, smem] + [anywhere] * 12,
        out_specs=(vmem, vmem),
        scratch_shapes=[
            pltpu.VMEM((7, HALF, HD), BF16),
            pltpu.VMEM((2 * HALF, HD), BF16),
            pltpu.VMEM((2 * HALF, HD), BF16),
            pltpu.VMEM((512, HALF), BF16),
            pltpu.VMEM((512, 1024), BF16),
            pltpu.VMEM((16, 256, HD), BF16),
            pltpu.VMEM((16, 256, HD), BF16),
            pltpu.VMEM((16, 1024), BF16),
            pltpu.VMEM((8, 16, 1024), BF16),
            pltpu.VMEM((TENANTS, HD), F32),
            pltpu.VMEM((TENANTS, 1024), F32),
            pltpu.VMEM((2, 128), jnp.int32),
            pltpu.VMEM((2, 128), jnp.int32),
            pltpu.VMEM((2, 128), jnp.int32),
            pltpu.VMEM((2, 128), jnp.int32),
            pltpu.VMEM((8, 512, HD), F32),
            pltpu.VMEM((8, TENANTS, HD), F32),
            pltpu.VMEM((15, 32, HD), F32),
            pltpu.VMEM((8, 128), F32),
            pltpu.VMEM((16, 8, 128), F32),
            pltpu.VMEM((16, 8, 128), F32),
            pltpu.VMEM((16, 8, 128), F32),
            pltpu.VMEM((128, HD), F32),
            pltpu.VMEM((128, 256), F32),
            pltpu.VMEM((128, HD), F32),
            pltpu.VMEM((128, 128), F32),
            pltpu.VMEM((TENANTS, 512), BF16),
            pltpu.VMEM((128, 128), F32),
            pltpu.VMEM((128, 128), F32),
            dma((12,)), dma, dma((4, ROUNDS)), dma((2, 7)), dma((4,)), dma((4,)), dma, dma((8,)),
            dma, dma, dma, dma, dma, dma, pltpu.SemaphoreType.REGULAR((4,)),
        ],
        compiler_params=pltpu.CompilerParams(
            collective_id=0, has_side_effects=True, vmem_limit_bytes=60 * 1024 * 1024
        ),
    )(
        cache_len, tenant_roll, roll_x, queries, cache_k, cache_v, w_key, w_value, ia3_key,
        ia3_value, train_x, upstream, tenant_train.reshape(2, 128), advantage.reshape(2, 128),
    )
    attn_out, gradient, tenant_loss = pl.pallas_call(
        outputs,
        out_shape=(
            jax.ShapeDtypeStruct((16, 1024), BF16),
            jax.ShapeDtypeStruct((2, 128), F32),
            jax.ShapeDtypeStruct((1, TENANTS), F32),
        ),
        in_specs=[vmem, vmem],
        out_specs=(vmem, vmem, vmem),
    )(*(pltpu.with_memory_space_constraint(a, pltpu.VMEM) for a in (attn, whole)))
    return attn_out, gradient, tenant_loss.reshape(TENANTS)


def solution(mesh):
    finer = Mesh(mesh.devices.reshape(2, 8, 2, 2, 4), AXES)
    placed = (
        P(DP, TENSOR), P(DP, TENSOR), P(DP, None, TENSOR), P(DP, None, TENSOR), P(DP), P(DP),
        P(None, TENSOR), P(None, TENSOR), P(), P(), P(DP_TENSOR, None), P(DP_TENSOR, None),
        P(DP_TENSOR), P(DP_TENSOR),
    )
    return jax.shard_map(
        local_step, mesh=finer, in_specs=placed, out_specs=(P(DP, TENSOR), P(DP, TENSOR), P()),
        check_vma=False,
    )
```

```python
import jax
import jax.numpy as jnp
from jax import lax
from jax.experimental import pallas as pl
from jax.experimental.pallas import tpu as pltpu
from jax.sharding import Mesh
from jax.sharding import PartitionSpec as P

HD = 128
TENANTS = 64
AXES = ("y_hi", "z", "core", "y_lo", "x")
DP = ("y_hi", "z", "core")
TENSOR = ("y_lo", "x")
DP_TENSOR = DP + TENSOR
MESH = pl.DeviceIdType.MESH
F32 = jnp.float32
BF16 = jnp.bfloat16

O, XM, XP, X2, F0, FM, FP, F2 = range(8)
SHIFT = ((0, 0), (0, 3), (0, 1), (0, 2), (1, 0), (1, 3), (1, 1), (1, 2))
INVERSE = (O, XP, XM, X2, F0, FP, FM, F2)

HALF = 4096
ZROWS = 1280
ZHALF = ZROWS // 2
QUARTER = ((0, 640), (640, 640), (1280, 768), (2048, 768))


def quarters(block, *which):
    return tuple((block, *QUARTER[k]) for k in which)


LINKS = (
    quarters(XM, 0, 1, 2, 3) + quarters(X2, 0, 2) + ((F2, 2816, 768), (F2, 3840, 256)),
    quarters(XP, 0, 1, 2, 3) + quarters(X2, 1, 3) + ((F2, 1280, 768), (F2, 3584, 256)),
    quarters(F0, 0, 2) + quarters(FM, 0, 1, 2, 3) + ((F2, 0, 640), (F2, 2048, 384)),
    quarters(F0, 1, 3) + quarters(FP, 0, 1, 2, 3) + ((F2, 640, 640), (F2, 2432, 384)),
)
ROUNDS = 8
SENT_AS = (
    {XM: O, X2: XM, F2: FM},
    {XP: O, X2: XP, F2: FP},
    {F0: O, FM: XM, FP: XP, F2: X2},
    {F0: O, FM: XM, FP: XP, F2: X2},
)
Z_SEND = {0: (F0,), 1: (XM, XP), 3: (FM, FP), 4: (X2,)}
Z_TAKE = {2: (F0,), 4: (XM, XP, FM), 5: (FP,), 6: (X2,)}
PRODUCTS = {
    1: (((O, F0), 0, 1280), ((XM, XP), 0, 640), ((O, F0), 1280, 1536), ((XM, XP), 640, 640)),
    2: (((XM, XP), 1280, 768), ((FM, FP), 0, 640), ((O, F0), 2816, 1280)),
    3: (((XM, XP), 2048, 768), ((FM, FP), 640, 640)),
    4: (((X2,), 0, 1280), ((FM, FP), 1280, 768), ((XM, XP), 2816, 1280)),
    5: (((X2,), 1280, 1536), ((FM, FP), 2048, 768), ((FM, FP), 2816, 1280)),
    6: (((X2,), 2816, 1280), ((F2,), 0, 2048), ((F2,), 2816, 768)),
    7: (((F2,), 2048, 768), ((F2,), 3584, 512)),
}
FINISH = {3: (O, F0), 4: (XM, XP), 5: (FM, FP), 6: (X2,), 7: (F2,)}
FAR_PLANE = (10, 2, 6, 8, 9, 11, 14, 1, 3, 4, 5, 7, 12, 13, 15)
FAR_COLUMN = (8, 9, 7, 6, 10, 5, 11, 4, 12, 3, 13, 2, 14, 1, 15)
AFTER_Z = ((0, 6), (1, 7))


def dot(a, b):
    return jnp.dot(a, b, preferred_element_type=F32)


def exact_dot(a, b, dims):
    return lax.dot_general(
        a, b, (dims, ((), ())), precision=lax.Precision.HIGHEST, preferred_element_type=F32
    )


def kernel(
    clen_h, troll_h, roll_h, q_h, ck_h, cv_h, wk_h, wv_h, ik_h, iv_h, x_h, up_h, tt_h, adv_h,
    attn_o, whole_o,
    clen, troll, wbuf, wv, wk, xh, up, kc, vc, q, rx, ik, iv, tt, adv, tt2, adv2, acc, sbuf, gbuf, lmine, lbuf,
    msg, rbuf, qs, sc, mix, snew, mt, lacc, cnt,
    lsem, wsend, wrecv, zrecv, xsend, xrecv, rsend, rrecv, gsend, grecv,
    lsend, lrecv, msend, mrecv, known,
):
    y_hi, z, core, y_lo, x = (lax.axis_index(a) for a in AXES)
    t = y_lo * 4 + x
    odd = z % 2
    y = 2 * y_hi + y_lo
    y_up, y_down = (y + 1) % 4, (y + 3) % 4
    sibling = (y_hi, z, 1 - core, y_lo, x)
    z_up = (y_hi, (z + 1) % 8, core, y_lo, x)
    z_down = (y_hi, (z + 7) % 8, core, y_lo, x)
    to_link = (
        (y_hi, z, core, y_lo, (x + 1) % 4),
        (y_hi, z, core, y_lo, (x + 3) % 4),
        (y_up // 2, z, core, y_up % 2, x),
        (y_down // 2, z, core, y_down % 2, x),
    )

    def place(block):
        return (y_lo + SHIFT[block][0]) % 2, (x + SHIFT[block][1]) % 4

    def peer(block):
        py, px = place(block)
        return (y_hi, z, core, py, px)

    def columns(block):
        py, px = place(block)
        return pl.ds(pl.multiple_of((py * 4 + px) * HD, HD), HD)

    def plane_peer(step):
        other = (y * 4 + x + step) % 16
        return other, (other // 8, z, core, (other // 4) % 2, other % 4)

    def column_peer(step):
        other = (z * 2 + core + step) % 16
        return other, (y_hi, other // 2, other % 2, y_lo, x)

    def remote(src, dst, send, recv, device):
        return pltpu.make_async_remote_copy(
            src_ref=src, dst_ref=dst, send_sem=send, recv_sem=recv,
            device_id=device, device_id_type=MESH,
        )

    own_half = pl.ds(pl.multiple_of(core * HALF, HALF), HALF)
    other_half = pl.ds(pl.multiple_of((1 - core) * HALF, HALF), HALF)
    local = [
        pltpu.make_async_copy(src, dst, lsem.at[k])
        for k, (src, dst) in enumerate(
            (
                (wv_h, wv),
                (x_h.at[:, own_half], xh.at[pl.ds(0, 256)]),
                (tt_h, tt),
                (adv_h, adv),
                (up_h, up.at[pl.ds(0, 256)]),
                (wk_h, wk),
                (roll_h, rx.at[t]),
                (ik_h.at[:, pl.ds(pl.multiple_of(t * HD, HD), HD)], ik),
                (iv_h, iv),
                (q_h, q),
                (ck_h, kc),
                (cv_h, vc),
                (clen_h, clen),
                (troll_h, troll),
            )
        )
    ]
    barrier = pltpu.get_barrier_semaphore()
    neighbours = to_link + (z_up, z_down, sibling)

    def tell(semaphore):
        for device in neighbours:
            pl.semaphore_signal(semaphore, inc=1, device_id=device, device_id_type=MESH)

    def hear(semaphore):
        pl.semaphore_wait(semaphore, len(neighbours))

    tell(barrier)
    for copy in local:
        copy.start()
    hear(barrier)

    def rows(first, length):
        return pl.multiple_of((1 - odd) * first + odd * (HALF - first - length), 128)

    def link_copy(link, r):
        block, first, length = LINKS[link][r]
        source = SENT_AS[link][block]
        row = rows(first, length)
        if source == O:
            src = wv_h.at[pl.ds(pl.multiple_of(core * HALF + row, 128), length)]
        else:
            src = wbuf.at[source - 1, pl.ds(row, length)]
        return remote(
            src, wbuf.at[block - 1, pl.ds(row, length)], wsend, wrecv.at[link, r], to_link[link]
        )

    def z_copy(block, h, base):
        ref = wbuf.at[block - 1, pl.ds(pl.multiple_of(base + h * ZHALF, 128), ZHALF)]
        return remote(ref, ref, wsend, zrecv.at[h, block - 1], z_up if h == 0 else z_down)

    z_sent = odd * (HALF - ZROWS)
    z_taken = (1 - odd) * (HALF - ZROWS)

    def issue(r):
        for link in range(4):
            if (link, r) not in AFTER_Z:
                link_copy(link, r).start()

    issue(0)
    issue(1)
    tell(known.at[0])
    exchange = [
        remote(src, dst, xsend.at[k], xrecv.at[k], sibling)
        for k, (src, dst) in enumerate(
            (
                (x_h.at[:, other_half], xh.at[pl.ds(256, 256)]),
                (up_h, up.at[pl.ds(256, 256)]),
                (tt_h, tt2),
                (adv_h, adv2),
            )
        )
    ]
    for copy in exchange:
        copy.start()
    beside_y = (y_hi, z, core, 1 - y_lo, x)
    RELAY = (
        ((0, O, 0, 1024), (1, O, 0, 1024), (4, O, 0, 1024)),
        ((0, XM, 0, 512), (1, XP, 512, 512), (0, F0, 0, 1024), (1, F0, 0, 1024)),
        ((4, X2, 0, 1024),),
    )

    def relay(step):
        copies = []
        for k, (to, block, first, width) in enumerate(RELAY[step]):
            py, px = place(block)
            here = py * 4 + px
            slot = rx.at[here, :, pl.ds(first, width)]
            source = roll_h if block == O else slot
            device = beside_y if to == 4 else to_link[to]
            copies.append(remote(source, slot, rsend, rrecv.at[3 * step + step // 2 + k], device))
        return copies

    for copy in relay(0):
        copy.start()

    def part_of(block, row, length):
        if block == O:
            return wv[pl.ds(pl.multiple_of(core * HALF + row, 128), length), :]
        return wbuf[block - 1, pl.ds(row, length), :]

    def product(blocks, first, length, new):
        row = rows(first, length)
        parts = [part_of(block, row, length) for block in blocks]
        both = parts[0] if len(parts) == 1 else jnp.concatenate(parts, axis=1)
        result = dot(xh[:, pl.ds(row, length)], both)
        for k, block in enumerate(blocks):
            if new:
                acc[block] = result[:, k * HD : (k + 1) * HD]
            else:
                acc[block] += result[:, k * HD : (k + 1) * HD]

    def sum_copies(block):
        copies = []
        for k, high in enumerate((y_hi, 1 - y_hi)):
            slot = INVERSE[block] + 8 * k
            if slot > 0:
                py, px = place(block)
                copies.append(
                    remote(
                        sbuf.at[block, pl.ds(pl.multiple_of(32 * high, 32), 32)],
                        gbuf.at[slot - 1], gsend, grecv, (high, z, core, py, px),
                    )
                )
        return copies

    def finish(block, first=False):
        weighted = acc[block] * up[:, columns(block)].astype(F32)
        high = weighted.astype(BF16)
        low = (weighted - high.astype(F32)).astype(BF16)
        sums = dot(mt[...], high) + dot(mt[...], low)
        sbuf[block] = sums
        for copy in sum_copies(block):
            copy.start()
        part = sums * iv[:, columns(block)]
        if first:
            lacc[0:64, :] = part
        else:
            lacc[0:64, :] += part

    def table():
        for k in (2, 3):
            local[k].wait()
        for k in (2, 3):
            exchange[k].wait_recv()
        tenant = lax.broadcasted_iota(jnp.int32, (64, 128), 0)
        hits = []
        for k in range(4):
            labels, gains = (tt, adv) if k < 2 else (tt2, adv2)
            k2 = k % 2
            hits.append(
                (tenant == jnp.broadcast_to(labels[k2 : k2 + 1, :], (64, 128))).astype(F32)
            )
            gain = jnp.broadcast_to(gains[k2 : k2 + 1, :].astype(F32), (64, 128))
            mt[:, k * 128 : (k + 1) * 128] = (hits[k] * gain).astype(BF16)
        cnt[0:64, :] = hits[0] + hits[1]
        cnt[64:128, :] = jnp.zeros((64, 128), F32)
        lacc[64:128, :] = jnp.zeros((64, 128), F32)

    scale = 1.0 / jnp.sqrt(F32(HD))

    def spread(h, transposed=False):
        shape = (16, 128) if transposed else (128, 16)
        pair = lax.broadcasted_iota(jnp.int32, shape, 1 if transposed else 0)
        row = lax.broadcasted_iota(jnp.int32, shape, 0 if transposed else 1)
        if h is None:
            return (pair // 8 == row).astype(F32).astype(BF16)
        return (pair == row * 8 + h).astype(F32).astype(BF16)

    def project():
        for k in (5, 6, 7, 9, 13):
            local[k].wait()
        relay(2)[0].wait_recv()
        key_sum = jnp.zeros((16, HD), F32)
        value_sum = jnp.zeros((16, HD), F32)
        for k in range(8):
            part = rx[k]
            key_sum = key_sum + dot(part, wk[k * 1024 : (k + 1) * 1024, :])
            value_sum = value_sum + dot(part, wv[k * 1024 : (k + 1) * 1024, :])
        row = lax.broadcasted_iota(jnp.int32, (16, TENANTS), 0)
        owner = jnp.zeros((16, TENANTS), jnp.int32)
        for r in range(16):
            owner = jnp.where(row == r, troll[r], owner)
        onehot = (owner == lax.broadcasted_iota(jnp.int32, (16, TENANTS), 1)).astype(F32)
        key_gain = exact_dot(onehot, ik[...], ((1,), (0,)))
        value_gain = exact_dot(onehot, iv[:, columns(O)], ((1,), (0,)))
        key_new = (key_sum * key_gain).astype(BF16)
        value_new = (value_sum * value_gain).astype(BF16)
        queries = jnp.zeros((128, HD), F32)
        for h in range(8):
            queries = queries + dot(spread(h), q[:, h * HD : (h + 1) * HD])
        qs[...] = queries
        each = spread(None)
        snew[...] = jnp.broadcast_to(
            jnp.sum(queries * dot(each, key_new), axis=1, keepdims=True) * scale, (128, 128)
        )
        mix[...] = dot(each, value_new)

    def score():
        local[10].wait()
        local[12].wait()
        place_in_cache = lax.broadcasted_iota(jnp.int32, (8, 256), 1)
        for r in range(16):
            s = lax.dot_general(
                qs[r * 8 : (r + 1) * 8, :].astype(BF16), kc[r], (((1,), (1,)), ((), ())),
                preferred_element_type=F32,
            ) * scale
            sc[r * 8 : (r + 1) * 8, :] = jnp.where(place_in_cache < clen[r], s, -jnp.inf)

    def normalise():
        s = sc[...]
        new = snew[:, 0:1]
        highest = jnp.maximum(jnp.max(s, axis=1, keepdims=True), new)
        expo = jnp.exp(s - highest)
        expo_new = jnp.exp(new - highest)
        denominator = jnp.sum(expo, axis=1, keepdims=True) + expo_new
        sc[...] = (expo / denominator).astype(BF16).astype(F32)
        mix[...] = (expo_new / denominator).astype(BF16).astype(F32) * mix[...]

    def mixture():
        local[11].wait()
        for r in range(16):
            rows = slice(r * 8, (r + 1) * 8)
            mix[rows, :] += dot(sc[rows, :].astype(BF16), vc[r])
        mixed = mix[...].astype(BF16)
        for h in range(8):
            attn_o[:, h * HD : (h + 1) * HD] = dot(spread(h, True), mixed).astype(BF16)

    ones = jnp.ones((8, 128), F32)
    pair_row = lax.broadcasted_iota(jnp.int32, (2, 128), 0)

    def loss_and_count():
        loss_row = exact_dot(ones, lacc[...], ((1,), (1,)))
        count_row = exact_dot(ones, cnt[...], ((1,), (1,)))
        return jnp.where(pair_row == 0, loss_row[0:2, :], count_row[0:2, :])

    beside = {2: project, 3: score, 4: normalise, 5: mixture}

    hear(known.at[0])
    tell(known.at[1])
    seen = set()
    for r in range(ROUNDS):
        for link in range(4):
            link_copy(link, r).wait_recv()
        if r + 2 < ROUNDS:
            issue(r + 2)
        for block in Z_SEND.get(r, ()):
            for h in range(2):
                z_copy(block, h, z_sent).start()
        if r < 3:
            hear(known.at[r + 1])
            if r < 2:
                tell(known.at[r + 2])
        if r < 2:
            for copy in relay(r):
                copy.wait_recv()
            for copy in relay(r + 1):
                copy.start()
        if r == 0:
            table()
            for k in (0, 1, 4, 8):
                local[k].wait()
        if r == 1:
            exchange[0].wait_recv()
            exchange[1].wait_recv()
        for block in Z_TAKE.get(r, ()):
            for h in range(2):
                z_copy(block, h, z_taken).wait_recv()
        for link, later in AFTER_Z:
            if later == r + 2:
                link_copy(link, later).start()
        for blocks, first, length in PRODUCTS.get(r, ()):
            product(blocks, first, length, blocks[0] not in seen)
            seen.update(blocks)
        if r in beside:
            beside[r]()
        for block in FINISH.get(r, ()):
            finish(block, block in (O, F2))
        if r == ROUNDS - 2:
            lmine[...] = loss_and_count()

    group = y * 4 + x
    mine = lmine[...] + jnp.where(
        pair_row == 0, exact_dot(ones, lacc[...], ((1,), (1,)))[0:2, :], 0.0
    )
    lmine[...] = mine
    for step in FAR_PLANE:
        remote(lmine, lbuf.at[group], lsend, lrecv, plane_peer(step)[1]).start()
    lbuf[group] = mine

    remote(gbuf, gbuf, gsend, grecv, sibling).wait_recv()
    total = sbuf[O, pl.ds(pl.multiple_of(32 * y_hi, 32), 32), :]
    for k in range(15):
        total = total + gbuf[k]
    remote(lbuf.at[pl.ds(0, 15)], lbuf.at[pl.ds(0, 15)], lsend, lrecv, sibling).wait_recv()
    plane = lbuf[0]
    for k in range(1, 16):
        plane = plane + lbuf[k]
    for k in range(16):
        msg[k, 0:2, :] = total[2 * k : 2 * k + 2, :]
        msg[k, 2:4, :] = plane
    own = z * 2 + core
    for step in FAR_COLUMN:
        other, device = column_peer(step)
        remote(msg.at[other], rbuf.at[own], msend, mrecv, device).start()
    rbuf[own] = msg[own]
    remote(rbuf.at[pl.ds(0, 15)], rbuf.at[pl.ds(0, 15)], msend, mrecv, sibling).wait_recv()
    whole = rbuf[0]
    for k in range(1, 16):
        whole = whole + rbuf[k]
    whole_o[...] = whole

    for copy in exchange:
        copy.wait_send()
    remote(rx.at[pl.ds(0, 7)], rx.at[pl.ds(0, 7)], rsend, grecv, sibling).wait_send()
    remote(wbuf, wbuf, wsend, grecv, sibling).wait_send()
    remote(gbuf, gbuf, gsend, grecv, sibling).wait_send()
    remote(lbuf.at[pl.ds(0, 15)], lbuf.at[pl.ds(0, 15)], lsend, lrecv, sibling).wait_send()
    remote(rbuf.at[pl.ds(0, 15)], rbuf.at[pl.ds(0, 15)], msend, mrecv, sibling).wait_send()


def outputs(attn, whole, attn_o, grad_o, loss_o):
    d = lax.axis_index("y_hi") * 16 + lax.axis_index("z") * 2 + lax.axis_index("core")
    attn_o[...] = attn[...]
    divisor = jnp.maximum(whole[3:4, :], 1.0)
    loss_o[...] = (-whole[2:3, :] / divisor)[:, 0:TENANTS]
    lane = lax.broadcasted_iota(jnp.int32, (2, 128), 1)
    row = lax.broadcasted_iota(jnp.int32, (2, 128), 0)
    own = jnp.sum(
        jnp.where(lane == 2 * d + row, jnp.broadcast_to(divisor, (2, 128)), 0.0),
        axis=1, keepdims=True,
    )
    grad_o[...] = -whole[0:2, :] / own


def local_step(
    roll_x, queries, cache_k, cache_v, cache_len, tenant_roll, w_key, w_value, ia3_key,
    ia3_value, train_x, upstream, tenant_train, advantage,
):
    vmem = pl.BlockSpec(memory_space=pltpu.VMEM)
    anywhere = pl.BlockSpec(memory_space=pl.ANY)
    dma = pltpu.SemaphoreType.DMA
    attn, whole = pl.pallas_call(
        kernel,
        out_shape=(
            pltpu.VMEM((16, 1024), BF16),
            pltpu.VMEM((4, 128), F32),
        ),
        in_specs=[anywhere] * 14,
        out_specs=(vmem, vmem),
        scratch_shapes=[
            pltpu.SMEM((16,), jnp.int32),
            pltpu.SMEM((16,), jnp.int32),
            pltpu.VMEM((7, HALF, HD), BF16),
            pltpu.VMEM((2 * HALF, HD), BF16),
            pltpu.VMEM((2 * HALF, HD), BF16),
            pltpu.VMEM((512, HALF), BF16),
            pltpu.VMEM((512, 1024), BF16),
            pltpu.VMEM((16, 256, HD), BF16),
            pltpu.VMEM((16, 256, HD), BF16),
            pltpu.VMEM((16, 1024), BF16),
            pltpu.VMEM((8, 16, 1024), BF16),
            pltpu.VMEM((TENANTS, HD), F32),
            pltpu.VMEM((TENANTS, 1024), F32),
            pltpu.VMEM((2, 128), jnp.int32),
            pltpu.VMEM((2, 128), jnp.int32),
            pltpu.VMEM((2, 128), jnp.int32),
            pltpu.VMEM((2, 128), jnp.int32),
            pltpu.VMEM((8, 512, HD), F32),
            pltpu.VMEM((8, TENANTS, HD), F32),
            pltpu.VMEM((15, 32, HD), F32),
            pltpu.VMEM((2, 128), F32),
            pltpu.VMEM((16, 2, 128), F32),
            pltpu.VMEM((16, 4, 128), F32),
            pltpu.VMEM((16, 4, 128), F32),
            pltpu.VMEM((128, HD), F32),
            pltpu.VMEM((128, 256), F32),
            pltpu.VMEM((128, HD), F32),
            pltpu.VMEM((128, 128), F32),
            pltpu.VMEM((TENANTS, 512), BF16),
            pltpu.VMEM((128, 128), F32),
            pltpu.VMEM((128, 128), F32),
            dma((14,)), dma, dma((4, ROUNDS)), dma((2, 7)), dma((4,)), dma((4,)), dma, dma((8,)),
            dma, dma, dma, dma, dma, dma, pltpu.SemaphoreType.REGULAR((4,)),
        ],
        compiler_params=pltpu.CompilerParams(
            collective_id=0, has_side_effects=True, vmem_limit_bytes=60 * 1024 * 1024
        ),
    )(
        cache_len, tenant_roll, roll_x, queries, cache_k, cache_v, w_key, w_value, ia3_key,
        ia3_value, train_x, upstream, tenant_train.reshape(2, 128), advantage.reshape(2, 128),
    )
    attn_out, gradient, tenant_loss = pl.pallas_call(
        outputs,
        out_shape=(
            jax.ShapeDtypeStruct((16, 1024), BF16),
            jax.ShapeDtypeStruct((2, 128), F32),
            jax.ShapeDtypeStruct((1, TENANTS), F32),
        ),
        in_specs=[vmem, vmem],
        out_specs=(vmem, vmem, vmem),
    )(*(pltpu.with_memory_space_constraint(a, pltpu.VMEM) for a in (attn, whole)))
    return attn_out, gradient, tenant_loss.reshape(TENANTS)


def solution(mesh):
    finer = Mesh(mesh.devices.reshape(2, 8, 2, 2, 4), AXES)
    placed = (
        P(DP, TENSOR), P(DP, TENSOR), P(DP, None, TENSOR), P(DP, None, TENSOR), P(DP), P(DP),
        P(None, TENSOR), P(None, TENSOR), P(), P(), P(DP_TENSOR, None), P(DP_TENSOR, None),
        P(DP_TENSOR), P(DP_TENSOR),
    )
    return jax.shard_map(
        local_step, mesh=finer, in_specs=placed, out_specs=(P(DP, TENSOR), P(DP, TENSOR), P()),
        check_vma=False,
    )
```

```python
import jax
import jax.numpy as jnp
from jax import lax
from jax.experimental import pallas as pl
from jax.experimental.pallas import tpu as pltpu
from jax.sharding import Mesh
from jax.sharding import PartitionSpec as P

HD = 128
TENANTS = 64
AXES = ("y_hi", "z", "core", "y_lo", "x")
DP = ("y_hi", "z", "core")
TENSOR = ("y_lo", "x")
DP_TENSOR = DP + TENSOR
MESH = pl.DeviceIdType.MESH
F32 = jnp.float32
BF16 = jnp.bfloat16

O, XM, XP, X2, F0, FM, FP, F2 = range(8)
SHIFT = ((0, 0), (0, 3), (0, 1), (0, 2), (1, 0), (1, 3), (1, 1), (1, 2))
INVERSE = (O, XP, XM, X2, F0, FP, FM, F2)

HALF = 4096
ZROWS = 1280
ZHALF = ZROWS // 2
QUARTER = ((0, 640), (640, 640), (1280, 768), (2048, 768))


def quarters(block, *which):
    return tuple((block, *QUARTER[k]) for k in which)


LINKS = (
    quarters(XM, 0, 1, 2, 3) + quarters(X2, 0, 2) + ((F2, 2816, 768), (F2, 3840, 256)),
    quarters(XP, 0, 1, 2, 3) + quarters(X2, 1, 3) + ((F2, 1280, 768), (F2, 3584, 256)),
    quarters(F0, 0, 2) + quarters(FM, 0, 1, 2, 3) + ((F2, 0, 640), (F2, 2048, 384)),
    quarters(F0, 1, 3) + quarters(FP, 0, 1, 2, 3) + ((F2, 640, 640), (F2, 2432, 384)),
)
ROUNDS = 8
SENT_AS = (
    {XM: O, X2: XM, F2: FM},
    {XP: O, X2: XP, F2: FP},
    {F0: O, FM: XM, FP: XP, F2: X2},
    {F0: O, FM: XM, FP: XP, F2: X2},
)
Z_SEND = {0: (F0,), 1: (XM, XP), 3: (FM, FP), 4: (X2,)}
Z_TAKE = {2: (F0,), 4: (XM, XP, FM), 5: (FP,), 6: (X2,)}
PRODUCTS = {
    1: (((O, F0), 0, 1280), ((XM, XP), 0, 640), ((O, F0), 1280, 1536), ((XM, XP), 640, 640)),
    2: (((XM, XP), 1280, 768), ((FM, FP), 0, 640), ((O, F0), 2816, 1280)),
    3: (((XM, XP), 2048, 768), ((FM, FP), 640, 640)),
    4: (((X2,), 0, 1280), ((FM, FP), 1280, 768), ((XM, XP), 2816, 1280)),
    5: (((X2,), 1280, 1536), ((FM, FP), 2048, 768), ((FM, FP), 2816, 1280)),
    6: (((X2,), 2816, 1280), ((F2,), 0, 2048), ((F2,), 2816, 768)),
    7: (((F2,), 2048, 768), ((F2,), 3584, 512)),
}
FINISH = {3: (O, F0), 4: (XM, XP), 5: (FM, FP), 6: (X2,), 7: (F2,)}
FAR_PLANE = (10, 2, 6, 8, 9, 11, 14, 1, 3, 4, 5, 7, 12, 13, 15)
FAR_COLUMN = (8, 9, 7, 6, 10, 5, 11, 4, 12, 3, 13, 2, 14, 1, 15)
AFTER_Z = ((0, 6), (1, 7))


def dot(a, b):
    return jnp.dot(a, b, preferred_element_type=F32)


def exact_dot(a, b, dims):
    return lax.dot_general(
        a, b, (dims, ((), ())), precision=lax.Precision.HIGHEST, preferred_element_type=F32
    )


def kernel(
    clen_h, troll_h, roll_h, q_h, ck_h, cv_h, wk_h, wv_h, ik_h, iv_h, x_h, up_h, tt_h, adv_h,
    attn_o, whole_o,
    clen, troll, wbuf, wv, wk, xh, up, kc, vc, q, rx, ik, iv, tt, adv, tt2, adv2, acc, sbuf, gbuf, lmine, lbuf,
    msg, rbuf, qs, sc, mix, snew, mt, lacc, cnt,
    lsem, wsend, wrecv, zrecv, xsend, xrecv, rsend, rrecv, gsend, grecv,
    lsend, lrecv, msend, mrecv, known,
):
    y_hi, z, core, y_lo, x = (lax.axis_index(a) for a in AXES)
    t = y_lo * 4 + x
    odd = z % 2
    y = 2 * y_hi + y_lo
    y_up, y_down = (y + 1) % 4, (y + 3) % 4
    sibling = (y_hi, z, 1 - core, y_lo, x)
    z_up = (y_hi, (z + 1) % 8, core, y_lo, x)
    z_down = (y_hi, (z + 7) % 8, core, y_lo, x)
    to_link = (
        (y_hi, z, core, y_lo, (x + 1) % 4),
        (y_hi, z, core, y_lo, (x + 3) % 4),
        (y_up // 2, z, core, y_up % 2, x),
        (y_down // 2, z, core, y_down % 2, x),
    )

    def place(block):
        return (y_lo + SHIFT[block][0]) % 2, (x + SHIFT[block][1]) % 4

    def peer(block):
        py, px = place(block)
        return (y_hi, z, core, py, px)

    def columns(block):
        py, px = place(block)
        return pl.ds(pl.multiple_of((py * 4 + px) * HD, HD), HD)

    def plane_peer(step):
        other = (y * 4 + x + step) % 16
        return other, (other // 8, z, core, (other // 4) % 2, other % 4)

    def column_peer(step):
        other = (z * 2 + core + step) % 16
        return other, (y_hi, other // 2, other % 2, y_lo, x)

    def remote(src, dst, send, recv, device):
        return pltpu.make_async_remote_copy(
            src_ref=src, dst_ref=dst, send_sem=send, recv_sem=recv,
            device_id=device, device_id_type=MESH,
        )

    own_half = pl.ds(pl.multiple_of(core * HALF, HALF), HALF)
    other_half = pl.ds(pl.multiple_of((1 - core) * HALF, HALF), HALF)
    local = [
        pltpu.make_async_copy(src, dst, lsem.at[k])
        for k, (src, dst) in enumerate(
            (
                (wv_h, wv),
                (x_h.at[:, own_half], xh.at[pl.ds(0, 256)]),
                (tt_h, tt),
                (adv_h, adv),
                (up_h, up.at[pl.ds(0, 256)]),
                (wk_h, wk),
                (roll_h, rx.at[t]),
                (ik_h.at[:, pl.ds(pl.multiple_of(t * HD, HD), HD)], ik),
                (iv_h, iv),
                (q_h, q),
                (ck_h, kc),
                (cv_h, vc),
                (clen_h, clen),
                (troll_h, troll),
            )
        )
    ]
    barrier = pltpu.get_barrier_semaphore()
    neighbours = to_link + (z_up, z_down, sibling)

    def tell(semaphore):
        for device in neighbours:
            pl.semaphore_signal(semaphore, inc=1, device_id=device, device_id_type=MESH)

    def hear(semaphore):
        pl.semaphore_wait(semaphore, len(neighbours))

    tell(barrier)
    for copy in local:
        copy.start()
    hear(barrier)

    def rows(first, length):
        return pl.multiple_of((1 - odd) * first + odd * (HALF - first - length), 128)

    def link_copy(link, r):
        block, first, length = LINKS[link][r]
        source = SENT_AS[link][block]
        row = rows(first, length)
        if source == O:
            src = wv_h.at[pl.ds(pl.multiple_of(core * HALF + row, 128), length)]
        else:
            src = wbuf.at[source - 1, pl.ds(row, length)]
        return remote(
            src, wbuf.at[block - 1, pl.ds(row, length)], wsend, wrecv.at[link, r], to_link[link]
        )

    def z_copy(block, h, base):
        ref = wbuf.at[block - 1, pl.ds(pl.multiple_of(base + h * ZHALF, 128), ZHALF)]
        return remote(ref, ref, wsend, zrecv.at[h, block - 1], z_up if h == 0 else z_down)

    z_sent = odd * (HALF - ZROWS)
    z_taken = (1 - odd) * (HALF - ZROWS)

    def issue(r):
        for link in range(4):
            if (link, r) not in AFTER_Z:
                link_copy(link, r).start()

    issue(0)
    issue(1)
    tell(known.at[0])
    exchange = [
        remote(src, dst, xsend.at[k], xrecv.at[k], sibling)
        for k, (src, dst) in enumerate(
            (
                (x_h.at[:, other_half], xh.at[pl.ds(256, 256)]),
                (up_h, up.at[pl.ds(256, 256)]),
                (tt_h, tt2),
                (adv_h, adv2),
            )
        )
    ]
    for copy in exchange:
        copy.start()
    beside_y = (y_hi, z, core, 1 - y_lo, x)
    RELAY = (
        ((0, O, 0, 1024), (1, O, 0, 1024), (4, O, 0, 1024)),
        ((0, XM, 0, 512), (1, XP, 512, 512), (0, F0, 0, 1024), (1, F0, 0, 1024)),
        ((4, X2, 0, 1024),),
    )

    def relay(step):
        copies = []
        for k, (to, block, first, width) in enumerate(RELAY[step]):
            py, px = place(block)
            here = py * 4 + px
            slot = rx.at[here, :, pl.ds(first, width)]
            source = roll_h if block == O else slot
            device = beside_y if to == 4 else to_link[to]
            copies.append(remote(source, slot, rsend, rrecv.at[3 * step + step // 2 + k], device))
        return copies

    for copy in relay(0):
        copy.start()

    def part_of(block, row, length):
        if block == O:
            return wv[pl.ds(pl.multiple_of(core * HALF + row, 128), length), :]
        return wbuf[block - 1, pl.ds(row, length), :]

    def product(blocks, first, length, new):
        row = rows(first, length)
        parts = [part_of(block, row, length) for block in blocks]
        both = parts[0] if len(parts) == 1 else jnp.concatenate(parts, axis=1)
        result = dot(xh[:, pl.ds(row, length)], both)
        for k, block in enumerate(blocks):
            if new:
                acc[block] = result[:, k * HD : (k + 1) * HD]
            else:
                acc[block] += result[:, k * HD : (k + 1) * HD]

    def sum_copies(block):
        copies = []
        for k, high in enumerate((y_hi, 1 - y_hi)):
            slot = INVERSE[block] + 8 * k
            if slot > 0:
                py, px = place(block)
                copies.append(
                    remote(
                        sbuf.at[block, pl.ds(pl.multiple_of(32 * high, 32), 32)],
                        gbuf.at[slot - 1], gsend, grecv, (high, z, core, py, px),
                    )
                )
        return copies

    def finish(block, first=False):
        weighted = acc[block] * up[:, columns(block)].astype(F32)
        high = weighted.astype(BF16)
        low = (weighted - high.astype(F32)).astype(BF16)
        sums = dot(mt[...], high) + dot(mt[...], low)
        sbuf[block] = sums
        for copy in sum_copies(block):
            copy.start()
        part = sums * iv[:, columns(block)]
        if first:
            lacc[0:64, :] = part
        else:
            lacc[0:64, :] += part

    def table():
        for k in (2, 3):
            local[k].wait()
        for k in (2, 3):
            exchange[k].wait_recv()
        tenant = lax.broadcasted_iota(jnp.int32, (64, 128), 0)
        hits = []
        for k in range(4):
            labels, gains = (tt, adv) if k < 2 else (tt2, adv2)
            k2 = k % 2
            hits.append(
                (tenant == jnp.broadcast_to(labels[k2 : k2 + 1, :], (64, 128))).astype(F32)
            )
            gain = jnp.broadcast_to(gains[k2 : k2 + 1, :].astype(F32), (64, 128))
            mt[:, k * 128 : (k + 1) * 128] = (hits[k] * gain).astype(BF16)
        cnt[0:64, :] = hits[0] + hits[1]
        cnt[64:128, :] = jnp.zeros((64, 128), F32)
        lacc[64:128, :] = jnp.zeros((64, 128), F32)

    scale = 1.0 / jnp.sqrt(F32(HD))

    def spread(h, transposed=False):
        shape = (16, 128) if transposed else (128, 16)
        pair = lax.broadcasted_iota(jnp.int32, shape, 1 if transposed else 0)
        row = lax.broadcasted_iota(jnp.int32, shape, 0 if transposed else 1)
        if h is None:
            return (pair // 8 == row).astype(F32).astype(BF16)
        return (pair == row * 8 + h).astype(F32).astype(BF16)

    def project():
        for k in (5, 6, 7, 9, 13):
            local[k].wait()
        relay(2)[0].wait_recv()
        key_sum = jnp.zeros((16, HD), F32)
        value_sum = jnp.zeros((16, HD), F32)
        for k in range(8):
            part = rx[k]
            key_sum = key_sum + dot(part, wk[k * 1024 : (k + 1) * 1024, :])
            value_sum = value_sum + dot(part, wv[k * 1024 : (k + 1) * 1024, :])
        row = lax.broadcasted_iota(jnp.int32, (16, TENANTS), 0)
        owner = jnp.zeros((16, TENANTS), jnp.int32)
        for r in range(16):
            owner = jnp.where(row == r, troll[r], owner)
        onehot = (owner == lax.broadcasted_iota(jnp.int32, (16, TENANTS), 1)).astype(F32)
        key_gain = exact_dot(onehot, ik[...], ((1,), (0,)))
        value_gain = exact_dot(onehot, iv[:, columns(O)], ((1,), (0,)))
        key_new = (key_sum * key_gain).astype(BF16)
        value_new = (value_sum * value_gain).astype(BF16)
        queries = jnp.zeros((128, HD), F32)
        for h in range(8):
            queries = queries + dot(spread(h), q[:, h * HD : (h + 1) * HD])
        qs[...] = queries
        each = spread(None)
        snew[...] = jnp.broadcast_to(
            jnp.sum(queries * dot(each, key_new), axis=1, keepdims=True) * scale, (128, 128)
        )
        mix[...] = dot(each, value_new)

    def score():
        local[10].wait()
        local[12].wait()
        place_in_cache = lax.broadcasted_iota(jnp.int32, (8, 256), 1)
        for r in range(16):
            s = lax.dot_general(
                qs[r * 8 : (r + 1) * 8, :].astype(BF16), kc[r], (((1,), (1,)), ((), ())),
                preferred_element_type=F32,
            ) * scale
            sc[r * 8 : (r + 1) * 8, :] = jnp.where(place_in_cache < clen[r], s, -jnp.inf)

    def normalise():
        s = sc[...]
        new = snew[:, 0:1]
        highest = jnp.maximum(jnp.max(s, axis=1, keepdims=True), new)
        expo = jnp.exp(s - highest)
        expo_new = jnp.exp(new - highest)
        denominator = jnp.sum(expo, axis=1, keepdims=True) + expo_new
        sc[...] = (expo / denominator).astype(BF16).astype(F32)
        mix[...] = (expo_new / denominator).astype(BF16).astype(F32) * mix[...]

    def mixture():
        local[11].wait()
        for r in range(16):
            rows = slice(r * 8, (r + 1) * 8)
            mix[rows, :] += dot(sc[rows, :].astype(BF16), vc[r])
        mixed = mix[...].astype(BF16)
        for h in range(8):
            attn_o[:, h * HD : (h + 1) * HD] = dot(spread(h, True), mixed).astype(BF16)

    ones = jnp.ones((8, 128), F32)
    pair_row = lax.broadcasted_iota(jnp.int32, (2, 128), 0)

    def loss_and_count():
        loss_row = exact_dot(ones, lacc[...], ((1,), (1,)))
        count_row = exact_dot(ones, cnt[...], ((1,), (1,)))
        return jnp.where(pair_row == 0, loss_row[0:2, :], count_row[0:2, :])

    beside = {2: project, 3: score, 4: normalise, 5: mixture}

    hear(known.at[0])
    tell(known.at[1])
    seen = set()
    for r in range(ROUNDS):
        for link in range(4):
            link_copy(link, r).wait_recv()
        for block in Z_SEND.get(r, ()):
            for h in range(2):
                z_copy(block, h, z_sent).start()
        if r + 2 < ROUNDS:
            issue(r + 2)
        if r < 3:
            hear(known.at[r + 1])
            if r < 2:
                tell(known.at[r + 2])
        if r < 2:
            for copy in relay(r):
                copy.wait_recv()
            for copy in relay(r + 1):
                copy.start()
        if r == 0:
            table()
            for k in (0, 1, 4, 8):
                local[k].wait()
        if r == 1:
            exchange[0].wait_recv()
            exchange[1].wait_recv()
        for block in Z_TAKE.get(r, ()):
            for h in range(2):
                z_copy(block, h, z_taken).wait_recv()
        for link, later in AFTER_Z:
            if later == r + 2:
                link_copy(link, later).start()
        for blocks, first, length in PRODUCTS.get(r, ()):
            product(blocks, first, length, blocks[0] not in seen)
            seen.update(blocks)
        if r in beside:
            beside[r]()
        for block in FINISH.get(r, ()):
            finish(block, block in (O, F2))
        if r == ROUNDS - 2:
            lmine[...] = loss_and_count()

    group = y * 4 + x
    mine = lmine[...] + jnp.where(
        pair_row == 0, exact_dot(ones, lacc[...], ((1,), (1,)))[0:2, :], 0.0
    )
    lmine[...] = mine
    for step in FAR_PLANE:
        remote(lmine, lbuf.at[group], lsend, lrecv, plane_peer(step)[1]).start()
    lbuf[group] = mine

    remote(gbuf, gbuf, gsend, grecv, sibling).wait_recv()
    total = sbuf[O, pl.ds(pl.multiple_of(32 * y_hi, 32), 32), :]
    for k in range(15):
        total = total + gbuf[k]
    remote(lbuf.at[pl.ds(0, 15)], lbuf.at[pl.ds(0, 15)], lsend, lrecv, sibling).wait_recv()
    plane = lbuf[0]
    for k in range(1, 16):
        plane = plane + lbuf[k]
    for k in range(16):
        msg[k, 0:2, :] = total[2 * k : 2 * k + 2, :]
        msg[k, 2:4, :] = plane
    own = z * 2 + core
    for step in FAR_COLUMN:
        other, device = column_peer(step)
        remote(msg.at[other], rbuf.at[own], msend, mrecv, device).start()
    rbuf[own] = msg[own]
    remote(rbuf.at[pl.ds(0, 15)], rbuf.at[pl.ds(0, 15)], msend, mrecv, sibling).wait_recv()
    whole = rbuf[0]
    for k in range(1, 16):
        whole = whole + rbuf[k]
    whole_o[...] = whole

    for copy in exchange:
        copy.wait_send()
    remote(rx.at[pl.ds(0, 7)], rx.at[pl.ds(0, 7)], rsend, grecv, sibling).wait_send()
    remote(wbuf, wbuf, wsend, grecv, sibling).wait_send()
    remote(gbuf, gbuf, gsend, grecv, sibling).wait_send()
    remote(lbuf.at[pl.ds(0, 15)], lbuf.at[pl.ds(0, 15)], lsend, lrecv, sibling).wait_send()
    remote(rbuf.at[pl.ds(0, 15)], rbuf.at[pl.ds(0, 15)], msend, mrecv, sibling).wait_send()


def outputs(attn, whole, attn_o, grad_o, loss_o):
    d = lax.axis_index("y_hi") * 16 + lax.axis_index("z") * 2 + lax.axis_index("core")
    attn_o[...] = attn[...]
    divisor = jnp.maximum(whole[3:4, :], 1.0)
    loss_o[...] = (-whole[2:3, :] / divisor)[:, 0:TENANTS]
    lane = lax.broadcasted_iota(jnp.int32, (2, 128), 1)
    row = lax.broadcasted_iota(jnp.int32, (2, 128), 0)
    own = jnp.sum(
        jnp.where(lane == 2 * d + row, jnp.broadcast_to(divisor, (2, 128)), 0.0),
        axis=1, keepdims=True,
    )
    grad_o[...] = -whole[0:2, :] / own


def local_step(
    roll_x, queries, cache_k, cache_v, cache_len, tenant_roll, w_key, w_value, ia3_key,
    ia3_value, train_x, upstream, tenant_train, advantage,
):
    vmem = pl.BlockSpec(memory_space=pltpu.VMEM)
    anywhere = pl.BlockSpec(memory_space=pl.ANY)
    dma = pltpu.SemaphoreType.DMA
    attn, whole = pl.pallas_call(
        kernel,
        out_shape=(
            pltpu.VMEM((16, 1024), BF16),
            pltpu.VMEM((4, 128), F32),
        ),
        in_specs=[anywhere] * 14,
        out_specs=(vmem, vmem),
        scratch_shapes=[
            pltpu.SMEM((16,), jnp.int32),
            pltpu.SMEM((16,), jnp.int32),
            pltpu.VMEM((7, HALF, HD), BF16),
            pltpu.VMEM((2 * HALF, HD), BF16),
            pltpu.VMEM((2 * HALF, HD), BF16),
            pltpu.VMEM((512, HALF), BF16),
            pltpu.VMEM((512, 1024), BF16),
            pltpu.VMEM((16, 256, HD), BF16),
            pltpu.VMEM((16, 256, HD), BF16),
            pltpu.VMEM((16, 1024), BF16),
            pltpu.VMEM((8, 16, 1024), BF16),
            pltpu.VMEM((TENANTS, HD), F32),
            pltpu.VMEM((TENANTS, 1024), F32),
            pltpu.VMEM((2, 128), jnp.int32),
            pltpu.VMEM((2, 128), jnp.int32),
            pltpu.VMEM((2, 128), jnp.int32),
            pltpu.VMEM((2, 128), jnp.int32),
            pltpu.VMEM((8, 512, HD), F32),
            pltpu.VMEM((8, TENANTS, HD), F32),
            pltpu.VMEM((15, 32, HD), F32),
            pltpu.VMEM((2, 128), F32),
            pltpu.VMEM((16, 2, 128), F32),
            pltpu.VMEM((16, 4, 128), F32),
            pltpu.VMEM((16, 4, 128), F32),
            pltpu.VMEM((128, HD), F32),
            pltpu.VMEM((128, 256), F32),
            pltpu.VMEM((128, HD), F32),
            pltpu.VMEM((128, 128), F32),
            pltpu.VMEM((TENANTS, 512), BF16),
            pltpu.VMEM((128, 128), F32),
            pltpu.VMEM((128, 128), F32),
            dma((14,)), dma, dma((4, ROUNDS)), dma((2, 7)), dma((4,)), dma((4,)), dma, dma((8,)),
            dma, dma, dma, dma, dma, dma, pltpu.SemaphoreType.REGULAR((4,)),
        ],
        compiler_params=pltpu.CompilerParams(
            collective_id=0, has_side_effects=True, vmem_limit_bytes=60 * 1024 * 1024
        ),
    )(
        cache_len, tenant_roll, roll_x, queries, cache_k, cache_v, w_key, w_value, ia3_key,
        ia3_value, train_x, upstream, tenant_train.reshape(2, 128), advantage.reshape(2, 128),
    )
    attn_out, gradient, tenant_loss = pl.pallas_call(
        outputs,
        out_shape=(
            jax.ShapeDtypeStruct((16, 1024), BF16),
            jax.ShapeDtypeStruct((2, 128), F32),
            jax.ShapeDtypeStruct((1, TENANTS), F32),
        ),
        in_specs=[vmem, vmem],
        out_specs=(vmem, vmem, vmem),
    )(*(pltpu.with_memory_space_constraint(a, pltpu.VMEM) for a in (attn, whole)))
    return attn_out, gradient, tenant_loss.reshape(TENANTS)


def solution(mesh):
    finer = Mesh(mesh.devices.reshape(2, 8, 2, 2, 4), AXES)
    placed = (
        P(DP, TENSOR), P(DP, TENSOR), P(DP, None, TENSOR), P(DP, None, TENSOR), P(DP), P(DP),
        P(None, TENSOR), P(None, TENSOR), P(), P(), P(DP_TENSOR, None), P(DP_TENSOR, None),
        P(DP_TENSOR), P(DP_TENSOR),
    )
    return jax.shard_map(
        local_step, mesh=finer, in_specs=placed, out_specs=(P(DP, TENSOR), P(DP, TENSOR), P()),
        check_vma=False,
    )
```
